256 devices in a mesh: wide: 32 (over y, z), narrow: 8 (over x, core).
Axes of the slice: x: 4, y: 4, z: 8, core: 2. Of those that a mesh axis runs over, the one named last changes fastest.
Arguments:
- step_one: bfloat16 [512, 18432], P('wide'), may hold values from -6 to 6
- step_two: bfloat16 [512, 18432], P('wide'), may hold values from -6 to 6
- gain: float32 [18432], replicated, may hold values from 0.1 to 1.9
- w_query: bfloat16 [18432, 12288], P('narrow', 'wide'), may hold values from -0.046875 to 0.046875
- w_keyval: bfloat16 [18432, 512], P('narrow', 'wide'), may hold values from -0.046875 to 0.046875
- w_out: bfloat16 [12288, 18432], P('wide', 'narrow'), may hold values from -0.4375 to 0.4375
- kv_cache: bfloat16 [512, 2048, 512], P(('wide', 'narrow'))
- lengths: int32 [512], P(('wide', 'narrow')), may hold values from 2 to 2048, as said below
Outputs:
- branch_one: bfloat16 [512, 18432], P('wide', 'narrow')
- branch_two: bfloat16 [512, 18432], P('wide', 'narrow')
The draws below stay inside these ranges and needn't reach their ends.
Inputs may be any that keep to these rules, and one draw needn't show every extreme that they name: `lengths`: at least one sequence has length 2048.
All inputs are finite; a program needn't handle non-finite values.
Results may differ from the reference program's by a relative error of at most 0.012.
Values may be sent and summed in bfloat16 or wider, within the bound.
No kernel may reach another device: no remote copies, remote signals or barrier semaphores. Data moves between devices by JAX's collectives and lax.ppermute only.
A program may use at most 64 MiB of HBM per device.

```python
import jax
import jax.numpy as jnp
from jax import lax

D = 18432
HEADS = 48
HD = 256
CACHE = 2048
BATCH_DEV = 2
BATCH = 512


def draw_kv_cache(key, part):
    key = jax.random.fold_in(key, 7)
    key_one = jax.random.fold_in(key, 0)
    entries = jax.random.normal(key_one, (BATCH, CACHE, 2 * HD), jnp.float32)
    return entries.astype(jnp.bfloat16)


def draw_lengths(key, part):
    key = jax.random.fold_in(key, 3)
    key_one, key_two = jax.random.split(key, 2)
    drawn = jax.random.randint(key_one, (BATCH,), 2, CACHE + 1)
    chosen = jax.random.randint(key_two, (), 0, BATCH)
    return jnp.where(jnp.arange(BATCH) == chosen, CACHE, drawn).astype(jnp.int32)


def block_scale(stream_key, shape, cuts, low, top_value):
    factor_of = 1.0
    for dim, shards_of in cuts:
        draws = jax.random.uniform(jax.random.fold_in(jax.random.fold_in(stream_key, 6), dim), (shards_of,), jnp.float32, low / len(cuts), top_value / len(cuts))
        factor_of = factor_of * jnp.repeat(jnp.exp(draws), shape[dim] // shards_of).reshape((-1,) + (1,) * (len(shape) - 1 - dim))
    return factor_of


def noise(stream_key, extent, spread, bound, shards=(), held_as=jnp.bfloat16):
    values = jax.random.normal(stream_key, extent, jnp.float32) * spread
    if len(shards) > 0:
        values = block_scale(stream_key, extent, shards, -0.22, 0.18) * values
    return jnp.clip(values, min=-bound, max=bound).astype(held_as)


def setup_inputs(seed: int = 0) -> dict:
    key_list = jax.random.split(jax.random.key(seed), 9)
    return {
        "step_one": noise(key_list[0], (BATCH, D), 1.0, 6.0, ((0, 32),)),
        "step_two": noise(key_list[1], (BATCH, D), 1.0, 6.0, ((0, 32),)),
        "gain": jnp.clip(1.0 + 0.18 * jax.random.normal(key_list[2], (D,), jnp.float32), 0.1, 1.9),
        "w_query": noise(key_list[3], (D, HEADS * HD), D ** -0.5, 0.046875, ((0, 8), (1, 32))),
        "w_keyval": noise(key_list[4], (D, 2 * HD), D ** -0.5, 0.046875, ((0, 8), (1, 32))),
        "w_out": noise(key_list[5], (HEADS * HD, D), (HEADS * HD // 64) ** -0.5, 0.4375, ((0, 32), (1, 8))),
        "kv_cache": draw_kv_cache(jax.random.fold_in(key_list[8], 71), 0),
        "lengths": draw_lengths(jax.random.fold_in(key_list[8], 71), 0),
    }


EPSILON = 1e-05
NEG_FILL = -1e+30

def normalize(inputs, gain):
    values = inputs.astype(jnp.float32)
    average = lax.optimization_barrier(jnp.mean(values, axis=-1, keepdims=True))
    variance = lax.optimization_barrier(jnp.mean(values * values, axis=-1, keepdims=True)) - average * average
    return ((values - average) * lax.rsqrt(variance + EPSILON) * gain.astype(jnp.float32)).astype(jnp.bfloat16)

def attend_block(block_items):
    queries, cache_block, row_lengths, new_keys, new_values = block_items
    rows_here = queries.shape[0]
    head_outputs = queries.reshape(rows_here, HEADS, HD).astype(jnp.float32)
    stored_key_rows = cache_block[:, :, :HD].astype(jnp.float32)
    stored_value_rows = cache_block[:, :, HD:].astype(jnp.float32)
    logit_scale_factor = HD ** (-0.5)
    attention_logits = jnp.einsum('xfw,xmw->xfm', head_outputs, stored_key_rows) * logit_scale_factor
    new_scores = jnp.einsum('bhd,bjd->bhj', head_outputs, new_keys.astype(jnp.float32)) * logit_scale_factor
    live_mask = jnp.arange(CACHE)[None, None, :] < row_lengths[:, None, None]
    attention_logits = jnp.where(live_mask, attention_logits, NEG_FILL)
    row_top = jnp.maximum(lax.optimization_barrier(jnp.max(attention_logits, axis=-1)), lax.optimization_barrier(jnp.max(new_scores, axis=-1)))
    stored_weight_matrix = jnp.where(live_mask, jnp.exp(attention_logits - row_top[..., None]), 0.0)
    new_weights = jnp.exp(new_scores - row_top[..., None])
    denominator = lax.optimization_barrier(jnp.sum(stored_weight_matrix, axis=-1)) + lax.optimization_barrier(jnp.sum(new_weights, axis=-1))
    weighted_value_sum = jnp.einsum('tiz,tzo->tio', stored_weight_matrix.astype(jnp.bfloat16).astype(jnp.float32), stored_value_rows)
    weighted_value_sum = weighted_value_sum + jnp.einsum('bhj,bjd->bhd', new_weights.astype(jnp.bfloat16).astype(jnp.float32), new_values.astype(jnp.float32))
    return (weighted_value_sum / denominator[..., None]).astype(jnp.bfloat16).reshape(rows_here, HEADS * HD)

def decode_layer(inputs, gain, w_query, w_keyval, w_out, kv_cache, lengths, earlier_keys, earlier_values):
    normed = normalize(inputs, gain)
    queries = jnp.dot(normed, w_query, preferred_element_type=jnp.float32).astype(jnp.bfloat16)
    keyval = jnp.dot(normed, w_keyval, preferred_element_type=jnp.float32).astype(jnp.bfloat16)
    new_keys = jnp.concatenate(earlier_keys + [keyval[:, None, :HD]], axis=1)
    new_values = jnp.concatenate(earlier_values + [keyval[:, None, HD:]], axis=1)
    blocks = BATCH // BATCH_DEV
    block_items = (queries.reshape(blocks, BATCH_DEV, HEADS * HD), kv_cache.reshape(blocks, BATCH_DEV, CACHE, 2 * HD), lengths.reshape(blocks, BATCH_DEV), new_keys.reshape(blocks, BATCH_DEV, new_keys.shape[1], HD), new_values.reshape(blocks, BATCH_DEV, new_values.shape[1], HD))
    attended = lax.map(attend_block, block_items).reshape(BATCH, HEADS * HD)
    branch = jnp.dot(attended, w_out, preferred_element_type=jnp.float32).astype(jnp.bfloat16)
    return (branch, keyval)

def reference(step_one, step_two, gain, w_query, w_keyval, w_out, kv_cache, lengths):
    branch_one, keyval_one = decode_layer(step_one, gain, w_query, w_keyval, w_out, kv_cache, lengths, [], [])
    branch_two, keyval_two = decode_layer(step_two, gain, w_query, w_keyval, w_out, kv_cache, lengths, [keyval_one[:, None, :HD]], [keyval_one[:, None, HD:]])
    return (branch_one, branch_two)
```

```python
import jax
import jax.numpy as jnp
from jax import lax
from jax.experimental import pallas as pl
from jax.experimental.pallas import tpu as pltpu
from jax.sharding import Mesh, PartitionSpec as P

HEADS = 48
EPSILON = 1e-05
NEG_FILL = -1e30
F32 = jnp.float32
BF16 = jnp.bfloat16


def normalize(inputs, gain, start, width):
    values = inputs.astype(F32)
    average = jnp.mean(values, axis=-1, keepdims=True)
    variance = jnp.mean(values * values, axis=-1, keepdims=True) - average * average
    own = lax.dynamic_slice_in_dim(inputs, start, width, 1).astype(F32)
    own_gain = lax.dynamic_slice_in_dim(gain, start, width, 0)
    return ((own - average) * lax.rsqrt(variance + EPSILON) * own_gain).astype(BF16)


def attend(queries, keyval, cache, lengths):
    steps, seqs, heads, size = queries.shape
    scale = size ** (-0.5)
    rows = queries.transpose(1, 0, 2, 3).reshape(seqs, steps * heads, size)
    keys, values = cache[:, :, :size], cache[:, :, size:]
    new = keyval.transpose(1, 0, 2)
    new_keys, new_values = new[:, :, :size], new[:, :, size:]
    live = (jnp.arange(cache.shape[1])[None, :] < lengths[:, None])[:, None, :]
    step_of = jnp.repeat(jnp.arange(steps), heads)
    new_live = (jnp.arange(steps)[None, :] <= step_of[:, None])[None]
    scores = jnp.einsum("srd,smd->srm", rows, keys, preferred_element_type=F32) * scale
    extra = jnp.einsum("srd,sjd->srj", rows, new_keys, preferred_element_type=F32) * scale
    scores = jnp.where(live, scores, NEG_FILL)
    extra = jnp.where(new_live, extra, NEG_FILL)
    top = jnp.maximum(jnp.max(scores, axis=-1), jnp.max(extra, axis=-1))[..., None]
    weights = jnp.where(live, jnp.exp(scores - top), 0.0)
    extra_weights = jnp.where(new_live, jnp.exp(extra - top), 0.0)
    total = jnp.sum(weights, axis=-1) + jnp.sum(extra_weights, axis=-1)
    out = jnp.einsum("srm,smd->srd", weights.astype(BF16), values, preferred_element_type=F32)
    out = out + jnp.einsum(
        "srj,sjd->srd", extra_weights.astype(BF16), new_values, preferred_element_type=F32
    )
    out = (out / total[..., None]).astype(BF16)
    return out.reshape(seqs, steps, heads * size).transpose(1, 0, 2)


def shift(value, axis, by):
    count = lax.axis_size(axis)
    return lax.ppermute(value, axis, [(i, (i + by) % count) for i in range(count)])


def add(*terms):
    return sum(t.astype(F32) for t in terms).astype(BF16)


def ring_gather(block, axis):
    half = lax.axis_size(axis) // 2
    up, down = [block], [block]
    for _ in range(half - 1):
        up.append(shift(up[-1], axis, 1))
        down.append(shift(down[-1], axis, -1))
    cut = block.shape[0] // 2
    far = jnp.concatenate([shift(up[-1][:cut], axis, 1), shift(down[-1][cut:], axis, -1)])
    return down + [far] + up[:0:-1]


def near_gather(block, axis):
    return [block] + [shift(block, axis, -k) for k in range(1, lax.axis_size(axis))]


def ring_scatter(stack, axis):
    count = lax.axis_size(axis)
    half = count // 2
    here = lax.axis_index(axis)

    def own(k):
        return lax.dynamic_index_in_dim(stack, lax.rem(here + k, count), 0, keepdims=False)

    far = own(half)
    cut = far.shape[0] // 2
    up, down = shift(far[:cut], axis, 1), shift(far[cut:], axis, -1)
    for k in range(half - 1, 0, -1):
        upper, lower = own(k), own(count - k)
        if k == half - 1:
            upper = jnp.concatenate([add(upper[:cut], up), upper[cut:]])
            lower = jnp.concatenate([lower[:cut], add(lower[cut:], down)])
        else:
            upper, lower = add(upper, up), add(lower, down)
        up, down = shift(upper, axis, 1), shift(lower, axis, -1)
    return add(own(0), up, down)


def near_scatter(stack, axis):
    count = lax.axis_size(axis)
    here = lax.axis_index(axis)
    own = [
        lax.dynamic_index_in_dim(stack, lax.rem(here + k, count), 0, keepdims=False)
        for k in range(count)
    ]
    return add(own[0], *(shift(own[k], axis, k) for k in range(1, count)))


def turn(value, dim, by):
    count = value.shape[dim]
    twice = jnp.concatenate([value, value], axis=dim)
    return lax.dynamic_slice_in_dim(twice, lax.rem(count - by, count), count, dim)


def ring_pieces(block, axis):
    half = lax.axis_size(axis) // 2
    up, down = [block], [block]
    for _ in range(half - 1):
        up.append(shift(up[-1], axis, 1))
        down.append(shift(down[-1], axis, -1))
    return down + [shift(up[-1], axis, 1)] + up[:0:-1]


def project_kernel(pieces, blocks, *refs):
    place_ref, refs = refs[0], refs[1:]
    row_refs, refs = refs[:pieces], refs[pieces:]
    weight_refs, refs = refs[:blocks], refs[blocks:]
    keyval_ref, keep_ref, give_ref, rows, sums, kept, given = refs
    here, core = place_ref[0], place_ref[1]
    nx, ny, out_rows, _ = keep_ref.shape
    depth, wide_cols = keyval_ref.shape[0], weight_refs[0].shape[1]
    per = out_rows // pieces
    part = nx * per
    count = row_refs[0].shape[0]
    group = sums.shape[0] // count
    for first in range(0, pieces, group):
        for p in range(group):
            rows[p * count : (p + 1) * count, :] = row_refs[first + p][...]
        for k in range(blocks):
            column = lax.rem(here + blocks - k, blocks) * wide_cols
            sums[:, pl.ds(pl.multiple_of(column, 128), wide_cols)] = jnp.dot(
                rows[...], weight_refs[k][:depth, :], preferred_element_type=F32
            )
        sums[:, blocks * wide_cols :] = jnp.dot(
            rows[...], keyval_ref[...], preferred_element_type=F32
        )
        for p in range(group):
            for y in range(ny):
                at = p * count + y * 2 * part
                mine = sums[pl.ds(pl.multiple_of(at + core * part, 8), part), :]
                theirs = sums[pl.ds(pl.multiple_of(at + (1 - core) * part, 8), part), :]
                slot = (first + p) * per
                for x in range(nx):
                    kept[x, y, slot : slot + per, :] = mine[x * per : (x + 1) * per]
                    given[x, y, slot : slot + per, :] = theirs[x * per : (x + 1) * per]
    for x in range(nx):
        keep_ref[x] = kept[x].astype(BF16)
        give_ref[x] = given[x].astype(BF16)


def project(place, pieces, weights, keyval, nx, per):
    blocks, cols = len(weights), weights[0].shape[1]
    depth = keyval.shape[0]
    count = pieces[0].shape[0]
    total = blocks * cols + keyval.shape[1]
    ny = count // (2 * nx * per)
    shape = (nx, ny, len(pieces) * per, total)
    group = len(pieces) // 2
    whole = pl.BlockSpec(memory_space=pltpu.VMEM)
    return pl.pallas_call(
        lambda *refs: project_kernel(len(pieces), blocks, *refs),
        in_specs=[pl.BlockSpec(memory_space=pltpu.SMEM)] + [whole] * (len(pieces) + blocks + 1),
        out_specs=[whole, whole],
        out_shape=[jax.ShapeDtypeStruct(shape, BF16)] * 2,
        scratch_shapes=[
            pltpu.VMEM((group * count, depth), BF16),
            pltpu.VMEM((group * count, total), F32),
            pltpu.VMEM(shape, F32),
            pltpu.VMEM(shape, F32),
        ],
        compiler_params=pltpu.CompilerParams(vmem_limit_bytes=40 * 2**20),
        cost_estimate=pl.CostEstimate(
            flops=2 * count * len(pieces) * depth * total,
            bytes_accessed=2 * total * (depth + count * len(pieces)),
            transcendentals=0,
        ),
    )(place, *pieces, *weights, keyval)


def shards(step_one, step_two, gain, w_query, w_keyval, w_out, kv_cache, lengths):
    ny, nz, nx, nc = (lax.axis_size(a) for a in ("y", "z", "x", "core"))
    wide, narrow = ny * nz, nx * nc
    here, core = lax.axis_index("y"), lax.axis_index("core")
    width, query_cols = w_query.shape
    pair_cols = w_keyval.shape[1]
    size = kv_cache.shape[2] // 2
    seqs = kv_cache.shape[0]
    per = 2 * seqs
    start = (lax.axis_index("x") * nc + core) * width
    depth = width // ny
    extra = depth * pair_cols // query_cols

    quarters = w_query.reshape(ny, depth, query_cols)
    smalls = w_keyval.reshape(ny, extra, query_cols)

    def quarter(k):
        at = lax.rem(here + k, ny)
        return jnp.concatenate(
            [
                lax.dynamic_index_in_dim(quarters, at, 0, keepdims=False),
                lax.dynamic_index_in_dim(smalls, at, 0, keepdims=False),
            ]
        )

    weights = [quarter(0)] + [shift(quarter(k), "y", k) for k in range(1, ny)]
    smalls = jnp.stack([w[depth:] for w in weights]).reshape(ny, depth, pair_cols)
    smalls = [
        lax.dynamic_index_in_dim(smalls, lax.rem(here + ny - i, ny), 0, keepdims=False)
        for i in range(ny)
    ]
    pad = jnp.zeros((depth, -ny * pair_cols % 128), BF16)
    keyval_weights = jnp.concatenate(smalls + [pad], axis=1)

    both = jnp.stack([normalize(s, gain, start, width) for s in (step_one, step_two)])
    mine = both.reshape(2, nx, nc, seqs, ny, depth).transpose(4, 2, 1, 0, 3, 5)
    mine = mine.reshape(ny, narrow * per, depth)
    column = lax.all_to_all(mine, "y", split_axis=0, concat_axis=0, tiled=True)
    pieces = ring_pieces(column.reshape(ny * narrow * per, depth), "z")
    place = jnp.stack([here, core]).astype(jnp.int32)
    keep, give = project(place, pieces, weights, keyval_weights, nx, per)
    cols = keep.shape[3]
    other = lax.ppermute(give, "core", [(0, 1), (1, 0)])
    pair = add(keep, other).reshape(nx * ny, nz * per, cols)
    terms = lax.all_to_all(pair, ("x", "y"), split_axis=0, concat_axis=0, tiled=True)
    summed = add(*(terms[i] for i in range(nx * ny))).reshape(nz, per, cols)
    summed = turn(summed, 0, lax.axis_index("z"))
    arrived = lax.all_to_all(summed, "z", split_axis=0, concat_axis=0, tiled=True)
    queries = arrived[:, :, : ny * query_cols].reshape(nz, per, ny, query_cols)
    queries = queries.transpose(1, 2, 0, 3).reshape(2, seqs, HEADS, size)
    keyval = arrived[:, :, ny * query_cols : ny * (query_cols + pair_cols)]
    keyval = keyval.reshape(nz, per, ny, pair_cols)
    keyval = keyval.transpose(1, 2, 0, 3).reshape(2, seqs, 2 * size)
    attended = attend(queries, keyval, kv_cache, lengths)
    leaving = attended.reshape(per, wide, query_cols).transpose(1, 0, 2)
    returned = lax.all_to_all(leaving, ("y", "z"), split_axis=0, concat_axis=0, tiled=True)
    returned = returned.reshape(wide * per, query_cols)
    copies = jnp.broadcast_to(returned, (nx, *returned.shape))
    gathered = lax.all_to_all(copies, "x", split_axis=0, concat_axis=0, tiled=True)
    gathered = lax.all_gather(gathered, "core", axis=0, tiled=False)
    gathered = gathered.reshape(nc, nx, ny, nz, per, query_cols).transpose(3, 2, 0, 1, 4, 5)
    gathered = gathered.reshape(wide * narrow * per, query_cols)
    out = jnp.dot(gathered, w_out, preferred_element_type=F32).astype(BF16)
    far = out.shape[1]
    out = lax.psum_scatter(out, "z", scatter_dimension=0, tiled=True)
    out = near_scatter(out.reshape(ny, narrow * per, far), "y")
    out = out.reshape(nc, nx, 2, seqs, far).transpose(2, 1, 0, 3, 4)
    out = out.reshape(2, narrow * seqs, far)
    return (out[0], out[1])


def solution(mesh):
    fine = Mesh(mesh.devices.reshape(4, 8, 4, 2), ("y", "z", "x", "core"))
    wide, narrow = ("y", "z"), ("x", "core")
    return jax.shard_map(
        shards,
        mesh=fine,
        in_specs=(
            P(wide, None),
            P(wide, None),
            P(),
            P(narrow, wide),
            P(narrow, wide),
            P(wide, narrow),
            P(wide + narrow, None, None),
            P(wide + narrow),
        ),
        out_specs=(P(wide, narrow), P(wide, narrow)),
        check_vma=False,
    )
```

```python
import jax
import jax.numpy as jnp
from jax import lax
from jax.experimental import pallas as pl
from jax.experimental.pallas import tpu as pltpu
from jax.sharding import Mesh, PartitionSpec as P

HEADS = 48
EPSILON = 1e-05
NEG_FILL = -1e30
F32 = jnp.float32
BF16 = jnp.bfloat16


def attend(queries, keyval, cache, lengths):
    steps, seqs, heads, size = queries.shape
    scale = size ** (-0.5)
    rows = queries.transpose(1, 0, 2, 3).reshape(seqs, steps * heads, size)
    keys, values = cache[:, :, :size], cache[:, :, size:]
    new = keyval.transpose(1, 0, 2)
    new_keys, new_values = new[:, :, :size], new[:, :, size:]
    live = (jnp.arange(cache.shape[1])[None, :] < lengths[:, None])[:, None, :]
    step_of = jnp.repeat(jnp.arange(steps), heads)
    new_live = (jnp.arange(steps)[None, :] <= step_of[:, None])[None]
    scores = jnp.einsum("srd,smd->srm", rows, keys, preferred_element_type=F32) * scale
    extra = jnp.einsum("srd,sjd->srj", rows, new_keys, preferred_element_type=F32) * scale
    scores = jnp.where(live, scores, NEG_FILL)
    extra = jnp.where(new_live, extra, NEG_FILL)
    top = jnp.maximum(jnp.max(scores, axis=-1), jnp.max(extra, axis=-1))[..., None]
    weights = jnp.where(live, jnp.exp(scores - top), 0.0)
    extra_weights = jnp.where(new_live, jnp.exp(extra - top), 0.0)
    total = jnp.sum(weights, axis=-1) + jnp.sum(extra_weights, axis=-1)
    out = jnp.einsum("srm,smd->srd", weights.astype(BF16), values, preferred_element_type=F32)
    out = out + jnp.einsum(
        "srj,sjd->srd", extra_weights.astype(BF16), new_values, preferred_element_type=F32
    )
    out = (out / total[..., None]).astype(BF16)
    return out.reshape(seqs, steps, heads * size).transpose(1, 0, 2)


VMEM = pl.BlockSpec(memory_space=pltpu.VMEM)
SMEM = pl.BlockSpec(memory_space=pltpu.SMEM)


def call(kernel, inputs, outputs, scratch, flops=0, mib=40):
    moved = sum(a.size * a.dtype.itemsize for a in (*inputs[1:], *outputs))
    return pl.pallas_call(
        kernel,
        in_specs=[SMEM] + [VMEM] * (len(inputs) - 1),
        out_specs=[VMEM] * len(outputs),
        out_shape=outputs,
        scratch_shapes=scratch,
        compiler_params=pltpu.CompilerParams(vmem_limit_bytes=mib * 2**20),
        cost_estimate=pl.CostEstimate(flops=flops, bytes_accessed=moved, transcendentals=0),
    )(*inputs)


def normalize(start, steps, gain, nx, nc, ny, width):
    count = steps[0].shape[0]
    seqs = count // (nx * nc)
    depth = width // ny

    def kernel(start_ref, one_ref, two_ref, gain_ref, out_ref, rows):
        columns = pl.ds(pl.multiple_of(start_ref[0], 128), width)
        scales = gain_ref[:, columns]
        for t, ref in enumerate((one_ref, two_ref)):
            values = ref[...].astype(F32)
            average = jnp.mean(values, axis=-1, keepdims=True)
            variance = jnp.mean(values * values, axis=-1, keepdims=True) - average * average
            own = ref[:, columns].astype(F32)
            normed = (own - average) * lax.rsqrt(variance + EPSILON) * scales
            for n in range(nx * nc):
                x, c = n // nc, n % nc
                at = ((c * nx + x) * 2 + t) * seqs
                rows[at : at + seqs, :] = normed[n * seqs : (n + 1) * seqs]
        for k in range(ny):
            out_ref[k] = rows[:, k * depth : (k + 1) * depth].astype(BF16)

    return call(
        kernel,
        (start, *steps, gain.reshape(1, -1)),
        [jax.ShapeDtypeStruct((ny, 2 * count, depth), BF16)],
        [pltpu.VMEM((2 * count, width), F32)],
    )[0]


def input_quarters(place, w_query, w_keyval, ny):
    width, cols = w_query.shape
    small = w_keyval.shape[1]
    depth = width // ny

    def kernel(place_ref, query_ref, keyval_ref, *out_refs):
        unit = (
            lax.broadcasted_iota(jnp.int32, (small, small), 0)
            == lax.broadcasted_iota(jnp.int32, (small, small), 1)
        ).astype(BF16)
        for k, out_ref in enumerate(out_refs):
            at = pl.multiple_of(lax.rem(place_ref[0] + k, ny) * depth, 16)
            out_ref[:depth, :] = query_ref[pl.ds(at, depth), :]
            turned = lax.dot_general(
                unit,
                keyval_ref[pl.ds(at, depth), :],
                (((1,), (1,)), ((), ())),
                preferred_element_type=F32,
            ).astype(BF16)
            rest = jnp.zeros((small, 2 * cols - depth), BF16)
            out_ref[depth : depth + small, :] = turned[:, :cols]
            out_ref[depth + small :, :] = jnp.concatenate([turned[:, cols:], rest], axis=1)

    shape = jax.ShapeDtypeStruct((depth + 2 * small, cols), BF16)
    return call(kernel, (place, w_query, w_keyval), [shape] * ny, [])


def output_quarters(place, w_out, ny):
    rows, width = w_out.shape
    depth = width // ny

    def kernel(place_ref, weights_ref, *refs):
        out_refs, quarters = refs[:-1], refs[-1]
        for k in range(ny):
            quarters[k] = weights_ref[:, k * depth : (k + 1) * depth]
        for k, out_ref in enumerate(out_refs):
            out_ref[...] = quarters[lax.rem(place_ref[0] + k, ny)]

    shape = jax.ShapeDtypeStruct((rows, depth), BF16)
    return call(kernel, (place, w_out), [shape] * ny, [pltpu.VMEM((ny, rows, depth), BF16)])


def shift(value, axis, by):
    count = lax.axis_size(axis)
    return lax.ppermute(value, axis, [(i, (i + by) % count) for i in range(count)])


def add(*terms):
    return sum(t.astype(F32) for t in terms).astype(BF16)


def ring_pieces(block, axis):
    half = lax.axis_size(axis) // 2
    up, down = [block], [block]
    for _ in range(half - 1):
        up.append(shift(up[-1], axis, 1))
        down.append(shift(down[-1], axis, -1))
    return down + [shift(up[-1], axis, 1)] + up[:0:-1]


def ring_sum(parts, axis):
    count = len(parts)
    half = count // 2
    up, down = shift(parts[half], axis, 1), None
    for k in range(half - 1, 0, -1):
        upper = add(parts[k], up)
        lower = parts[count - k] if down is None else add(parts[count - k], down)
        up, down = shift(upper, axis, 1), shift(lower, axis, -1)
    return add(parts[0], up, down)


def project(place, pieces, weights, small, nx, per):
    count, depth = pieces[0].shape
    ny, cols = len(weights), weights[0].shape[1]
    nz = len(pieces)
    part = nx * per
    total = ny * cols + 128
    shape = (nx, ny, nz * per, total)
    group = nz // 2

    def kernel(place_ref, *refs):
        row_refs, refs = refs[:nz], refs[nz:]
        weight_refs, refs = refs[:ny], refs[ny:]
        keep_ref, give_ref, rows, smalls, sums, kept, given = refs
        here, core = place_ref[0], place_ref[1]
        smalls[...] = jnp.zeros_like(smalls)
        for k in range(ny):
            to = pl.ds(pl.multiple_of(lax.rem(here + ny - k, ny) * small, 16), small)
            smalls[to, :cols] = weight_refs[k][depth : depth + small, :]
            smalls[to, cols:] = weight_refs[k][depth + small :, : depth - cols]
        for first in range(0, nz, group):
            for p in range(group):
                rows[p * count : (p + 1) * count, :] = row_refs[first + p][...]
            for k in range(ny):
                to = pl.multiple_of(lax.rem(here + ny - k, ny) * cols, 128)
                sums[:, pl.ds(to, cols)] = jnp.dot(
                    rows[...], weight_refs[k][:depth, :], preferred_element_type=F32
                )
            sums[:, ny * cols :] = lax.dot_general(
                rows[...], smalls[...], (((1,), (1,)), ((), ())), preferred_element_type=F32
            )
            for p in range(group):
                for y in range(ny):
                    at = p * count + y * 2 * part
                    mine = sums[pl.ds(pl.multiple_of(at + core * part, 8), part), :]
                    theirs = sums[pl.ds(pl.multiple_of(at + (1 - core) * part, 8), part), :]
                    slot = (first + p) * per
                    for x in range(nx):
                        kept[x, y, slot : slot + per, :] = mine[x * per : (x + 1) * per]
                        given[x, y, slot : slot + per, :] = theirs[x * per : (x + 1) * per]
        for x in range(nx):
            keep_ref[x] = kept[x].astype(BF16)
            give_ref[x] = given[x].astype(BF16)

    return call(
        kernel,
        (place, *pieces, *weights),
        [jax.ShapeDtypeStruct(shape, BF16)] * 2,
        [
            pltpu.VMEM((group * count, depth), BF16),
            pltpu.VMEM((128, depth), BF16),
            pltpu.VMEM((group * count, total), F32),
            pltpu.VMEM(shape, F32),
            pltpu.VMEM(shape, F32),
        ],
        flops=2 * count * nz * depth * total,
    )


def sum_terms(place, terms, per):
    def kernel(place_ref, terms_ref, out_ref):
        total = terms_ref[0].astype(F32)
        for i in range(1, terms_ref.shape[0]):
            total = total + terms_ref[i].astype(F32)
        out_ref[...] = pltpu.roll(total, place_ref[2] * per, 0).astype(BF16)

    return call(kernel, (place, terms), [jax.ShapeDtypeStruct(terms.shape[1:], BF16)], [])[0]


def project_out(place, own, other, weights, nx, nc, seqs):
    groups, count, width = own.shape
    ny = len(weights)
    rows, depth = weights[0].shape
    per = 2 * seqs
    nz = count // per
    block = ny * 2 * nx * nc * seqs

    def kernel(place_ref, own_ref, other_ref, *refs):
        weight_refs, refs = refs[:ny], refs[ny:]
        out_refs, (sums, slots) = refs[:nz], refs[nz:]
        here, core, depth_at = place_ref[0], place_ref[1], place_ref[2]
        for c in range(nc):
            for k in range(ny):
                at = pl.ds(pl.multiple_of(lax.rem(here + ny - k, ny) * rows, 128), rows)
                piece = jnp.where(core == c, own_ref[:, :, at], other_ref[:, :, at])
                term = jnp.dot(
                    piece.reshape(groups * count, rows),
                    weight_refs[k][...],
                    preferred_element_type=F32,
                )
                if k == 0:
                    sums[...] = term
                else:
                    sums[...] += term
            for x in range(nx):
                for y in range(ny):
                    for z in range(nz):
                        for t in range(2):
                            at = (x * ny + y) * count + z * per + t * seqs
                            to = ((y * 2 + t) * nx * nc + x * nc + c) * seqs
                            slots[z, to : to + seqs, :] = sums[at : at + seqs, :]
        for k in range(nz):
            out_refs[k][...] = slots[lax.rem(depth_at + k, nz)].astype(BF16)

    return call(
        kernel,
        (place, own, other, *weights),
        [jax.ShapeDtypeStruct((block, depth), BF16)] * nz,
        [pltpu.VMEM((groups * count, depth), F32), pltpu.VMEM((nz, block, depth), F32)],
        flops=2 * nc * groups * count * width * depth,
    )


def join_columns(place, blocks):
    count, rows, depth = blocks.shape

    def kernel(place_ref, blocks_ref, one_ref, two_ref, joined):
        for k in range(count):
            joined[:, k * depth : (k + 1) * depth] = blocks_ref[k].astype(F32)
        one_ref[...] = joined[: rows // 2, :].astype(BF16)
        two_ref[...] = joined[rows // 2 :, :].astype(BF16)

    shape = jax.ShapeDtypeStruct((rows // 2, count * depth), BF16)
    return call(kernel, (place, blocks), [shape] * 2, [pltpu.VMEM((rows, count * depth), F32)])


def shards(step_one, step_two, gain, w_query, w_keyval, w_out, kv_cache, lengths):
    ny, nz, nx, nc = (lax.axis_size(a) for a in ("y", "z", "x", "core"))
    narrow = nx * nc
    places = [lax.axis_index(a) for a in ("y", "core", "z", "x")]
    place = jnp.stack(places).astype(jnp.int32)
    width, query_cols = w_query.shape
    pair_cols = w_keyval.shape[1]
    size = kv_cache.shape[2] // 2
    seqs = kv_cache.shape[0]
    per = 2 * seqs
    depth = width // ny

    quarters = input_quarters(place, w_query, w_keyval, ny)
    weights = [quarters[0]] + [shift(quarters[k], "y", k) for k in range(1, ny)]

    quarters = output_quarters(place, w_out, ny)
    out_weights = [quarters[0]] + [shift(quarters[k], "y", k) for k in range(1, ny)]

    start = ((places[3] * nc + places[1]) * width).astype(jnp.int32).reshape(1)
    mine = normalize(start, (step_one, step_two), gain, nx, nc, ny, width)
    column = lax.all_to_all(mine, "y", split_axis=0, concat_axis=0, tiled=True)
    pieces = ring_pieces(column.reshape(ny * narrow * per, depth), "z")
    keep, give = project(place, pieces, weights, pair_cols, nx, per)
    cols = keep.shape[3]
    other = lax.ppermute(give, "core", [(0, 1), (1, 0)])
    pair = add(keep, other).reshape(nx * ny, nz * per, cols)
    pair, out_weights = lax.optimization_barrier((pair, out_weights))
    terms = lax.all_to_all(pair, ("x", "y"), split_axis=0, concat_axis=0, tiled=True)
    summed = sum_terms(place, terms, per)
    arrived = lax.all_to_all(
        summed.reshape(nz, per, cols), "z", split_axis=0, concat_axis=0, tiled=True
    )
    queries = arrived[:, :, : ny * query_cols].reshape(nz, per, ny, query_cols)
    queries = queries.transpose(1, 2, 0, 3).reshape(2, seqs, HEADS, size)
    keyval = arrived[:, :, ny * query_cols : ny * (query_cols + pair_cols)]
    keyval = keyval.reshape(nz, per, ny, pair_cols)
    keyval = keyval.transpose(1, 2, 0, 3).reshape(2, seqs, 2 * size)
    attended = attend(queries, keyval, kv_cache, lengths)
    leaving = attended.reshape(per, ny, nz, query_cols).transpose(2, 0, 1, 3)
    leaving = leaving.reshape(nz, per, ny * query_cols)
    returned = lax.all_to_all(leaving, "z", split_axis=0, concat_axis=0, tiled=True)
    returned = returned.reshape(nz * per, ny * query_cols)
    copies = jnp.broadcast_to(returned, (nx * ny, *returned.shape))
    gathered = lax.all_to_all(copies, ("x", "y"), split_axis=0, concat_axis=0, tiled=True)
    other = lax.ppermute(gathered, "core", [(0, 1), (1, 0)])
    parts = project_out(place, gathered, other, out_weights, nx, nc, seqs)
    out = ring_sum(parts, "z").reshape(ny, narrow * per, depth)
    out = lax.all_to_all(out, "y", split_axis=0, concat_axis=0, tiled=True)
    return tuple(join_columns(place, out))


def solution(mesh):
    fine = Mesh(mesh.devices.reshape(4, 8, 4, 2), ("y", "z", "x", "core"))
    wide, narrow = ("y", "z"), ("x", "core")
    return jax.shard_map(
        shards,
        mesh=fine,
        in_specs=(
            P(wide, None),
            P(wide, None),
            P(),
            P(narrow, wide),
            P(narrow, wide),
            P(wide, narrow),
            P(wide + narrow, None, None),
            P(wide + narrow),
        ),
        out_specs=(P(wide, narrow), P(wide, narrow)),
        check_vma=False,
    )
```

```python
import jax
import jax.numpy as jnp
from jax import lax
from jax.experimental import pallas as pl
from jax.experimental.pallas import tpu as pltpu
from jax.sharding import Mesh, PartitionSpec as P

HEADS = 48
EPSILON = 1e-05
NEG_FILL = -1e30
F32 = jnp.float32
BF16 = jnp.bfloat16


def attend(queries, keyval, cache, lengths):
    steps, seqs, heads, size = queries.shape
    scale = size ** (-0.5)
    rows = queries.transpose(1, 0, 2, 3).reshape(seqs, steps * heads, size)
    keys, values = cache[:, :, :size], cache[:, :, size:]
    new = keyval.transpose(1, 0, 2)
    new_keys, new_values = new[:, :, :size], new[:, :, size:]
    live = (jnp.arange(cache.shape[1])[None, :] < lengths[:, None])[:, None, :]
    step_of = jnp.repeat(jnp.arange(steps), heads)
    new_live = (jnp.arange(steps)[None, :] <= step_of[:, None])[None]
    scores = jnp.einsum("srd,smd->srm", rows, keys, preferred_element_type=F32) * scale
    extra = jnp.einsum("srd,sjd->srj", rows, new_keys, preferred_element_type=F32) * scale
    scores = jnp.where(live, scores, NEG_FILL)
    extra = jnp.where(new_live, extra, NEG_FILL)
    top = jnp.maximum(jnp.max(scores, axis=-1), jnp.max(extra, axis=-1))[..., None]
    weights = jnp.where(live, jnp.exp(scores - top), 0.0)
    extra_weights = jnp.where(new_live, jnp.exp(extra - top), 0.0)
    total = jnp.sum(weights, axis=-1) + jnp.sum(extra_weights, axis=-1)
    out = jnp.einsum("srm,smd->srd", weights.astype(BF16), values, preferred_element_type=F32)
    out = out + jnp.einsum(
        "srj,sjd->srd", extra_weights.astype(BF16), new_values, preferred_element_type=F32
    )
    out = (out / total[..., None]).astype(BF16)
    return out.reshape(seqs, steps, heads * size).transpose(1, 0, 2)


VMEM = pl.BlockSpec(memory_space=pltpu.VMEM)
SMEM = pl.BlockSpec(memory_space=pltpu.SMEM)


def call(kernel, inputs, outputs, scratch, flops=0, mib=40):
    moved = sum(a.size * a.dtype.itemsize for a in (*inputs[1:], *outputs))
    return pl.pallas_call(
        kernel,
        in_specs=[SMEM] + [VMEM] * (len(inputs) - 1),
        out_specs=[VMEM] * len(outputs),
        out_shape=outputs,
        scratch_shapes=scratch,
        compiler_params=pltpu.CompilerParams(vmem_limit_bytes=mib * 2**20),
        cost_estimate=pl.CostEstimate(flops=flops, bytes_accessed=moved, transcendentals=0),
    )(*inputs)


def normalize(start, steps, gain, nx, nc, ny, width):
    count = steps[0].shape[0]
    seqs = count // (nx * nc)
    depth = width // ny

    def kernel(start_ref, one_ref, two_ref, gain_ref, out_ref, rows):
        columns = pl.ds(pl.multiple_of(start_ref[0], 128), width)
        scales = gain_ref[:, columns]
        for t, ref in enumerate((one_ref, two_ref)):
            values = ref[...].astype(F32)
            average = jnp.mean(values, axis=-1, keepdims=True)
            variance = jnp.mean(values * values, axis=-1, keepdims=True) - average * average
            own = ref[:, columns].astype(F32)
            normed = (own - average) * lax.rsqrt(variance + EPSILON) * scales
            for n in range(nx * nc):
                x, c = n // nc, n % nc
                at = ((c * nx + x) * 2 + t) * seqs
                rows[at : at + seqs, :] = normed[n * seqs : (n + 1) * seqs]
        for k in range(ny):
            out_ref[k] = rows[:, k * depth : (k + 1) * depth].astype(BF16)

    return call(
        kernel,
        (start, *steps, gain.reshape(1, -1)),
        [jax.ShapeDtypeStruct((ny, 2 * count, depth), BF16)],
        [pltpu.VMEM((2 * count, width), F32)],
        mib=58,
    )[0]


def input_quarters(place, w_query, w_keyval, ny):
    width, cols = w_query.shape
    small = w_keyval.shape[1]
    depth = width // ny

    def kernel(place_ref, query_ref, keyval_ref, *out_refs):
        unit = (
            lax.broadcasted_iota(jnp.int32, (small, small), 0)
            == lax.broadcasted_iota(jnp.int32, (small, small), 1)
        ).astype(BF16)
        for k, out_ref in enumerate(out_refs):
            at = pl.multiple_of(lax.rem(place_ref[0] + k, ny) * depth, 16)
            out_ref[:depth, :] = query_ref[pl.ds(at, depth), :]
            turned = lax.dot_general(
                unit,
                keyval_ref[pl.ds(at, depth), :],
                (((1,), (1,)), ((), ())),
                preferred_element_type=F32,
            ).astype(BF16)
            rest = jnp.zeros((small, 2 * cols - depth), BF16)
            out_ref[depth : depth + small, :] = turned[:, :cols]
            out_ref[depth + small :, :] = jnp.concatenate([turned[:, cols:], rest], axis=1)

    shape = jax.ShapeDtypeStruct((depth + 2 * small, cols), BF16)
    return call(kernel, (place, w_query, w_keyval), [shape] * ny, [])


def output_quarters(place, w_out, ny):
    rows, width = w_out.shape
    depth = width // ny

    def kernel(place_ref, weights_ref, *refs):
        out_refs, quarters = refs[:-1], refs[-1]
        for k in range(ny):
            quarters[k] = weights_ref[:, k * depth : (k + 1) * depth]
        for k, out_ref in enumerate(out_refs):
            out_ref[...] = quarters[lax.rem(place_ref[0] + k, ny)]

    shape = jax.ShapeDtypeStruct((rows, depth), BF16)
    return call(kernel, (place, w_out), [shape] * ny, [pltpu.VMEM((ny, rows, depth), BF16)])


def shift(value, axis, by):
    count = lax.axis_size(axis)
    return lax.ppermute(value, axis, [(i, (i + by) % count) for i in range(count)])


def add(*terms):
    return sum(t.astype(F32) for t in terms).astype(BF16)


def ring_pieces(block, axis):
    half = lax.axis_size(axis) // 2
    up, down = [block], [block]
    for _ in range(half - 1):
        up.append(shift(up[-1], axis, 1))
        down.append(shift(down[-1], axis, -1))
    return down + [shift(up[-1], axis, 1)] + up[:0:-1]


def ring_sum(parts, axis):
    count = len(parts)
    half = count // 2
    up, down = shift(parts[half], axis, 1), None
    for k in range(half - 1, 0, -1):
        upper = add(parts[k], up)
        lower = parts[count - k] if down is None else add(parts[count - k], down)
        up, down = shift(upper, axis, 1), shift(lower, axis, -1)
    return add(parts[0], up, down)


def project(place, pieces, weights, small, nx, per):
    count, depth = pieces[0].shape
    ny, cols = len(weights), weights[0].shape[1]
    nz = len(pieces)
    part = nx * per
    total = ny * cols + 128
    shape = (nx, ny, nz * per, total)
    group = nz // 2

    def kernel(place_ref, *refs):
        row_refs, refs = refs[:nz], refs[nz:]
        weight_refs, refs = refs[:ny], refs[ny:]
        keep_ref, give_ref, rows, smalls, sums, kept, given = refs
        here, core = place_ref[0], place_ref[1]
        smalls[...] = jnp.zeros_like(smalls)
        for k in range(ny):
            to = pl.ds(pl.multiple_of(lax.rem(here + ny - k, ny) * small, 16), small)
            smalls[to, :cols] = weight_refs[k][depth : depth + small, :]
            smalls[to, cols:] = weight_refs[k][depth + small :, : depth - cols]
        for first in range(0, nz, group):
            for p in range(group):
                rows[p * count : (p + 1) * count, :] = row_refs[first + p][...]
            for k in range(ny):
                to = pl.multiple_of(lax.rem(here + ny - k, ny) * cols, 128)
                sums[:, pl.ds(to, cols)] = jnp.dot(
                    rows[...], weight_refs[k][:depth, :], preferred_element_type=F32
                )
            sums[:, ny * cols :] = lax.dot_general(
                rows[...], smalls[...], (((1,), (1,)), ((), ())), preferred_element_type=F32
            )
            for p in range(group):
                for y in range(ny):
                    at = p * count + y * 2 * part
                    mine = sums[pl.ds(pl.multiple_of(at + core * part, 8), part), :]
                    theirs = sums[pl.ds(pl.multiple_of(at + (1 - core) * part, 8), part), :]
                    slot = (first + p) * per
                    for x in range(nx):
                        kept[x, y, slot : slot + per, :] = mine[x * per : (x + 1) * per]
                        given[x, y, slot : slot + per, :] = theirs[x * per : (x + 1) * per]
        for x in range(nx):
            keep_ref[x] = kept[x].astype(BF16)
            give_ref[x] = given[x].astype(BF16)

    return call(
        kernel,
        (place, *pieces, *weights),
        [jax.ShapeDtypeStruct(shape, BF16)] * 2,
        [
            pltpu.VMEM((group * count, depth), BF16),
            pltpu.VMEM((128, depth), BF16),
            pltpu.VMEM((group * count, total), F32),
            pltpu.VMEM(shape, F32),
            pltpu.VMEM(shape, F32),
        ],
        flops=2 * count * nz * depth * total,
    )


def sum_terms(place, terms, per):
    def kernel(place_ref, terms_ref, out_ref):
        total = terms_ref[0].astype(F32)
        for i in range(1, terms_ref.shape[0]):
            total = total + terms_ref[i].astype(F32)
        out_ref[...] = pltpu.roll(total, place_ref[2] * per, 0).astype(BF16)

    return call(kernel, (place, terms), [jax.ShapeDtypeStruct(terms.shape[1:], BF16)], [])[0]


def project_out(place, own, other, weights, nx, nc, seqs):
    groups, count, width = own.shape
    ny = len(weights)
    rows, depth = weights[0].shape
    per = 2 * seqs
    nz = count // per
    block = ny * 2 * nx * nc * seqs

    def kernel(place_ref, own_ref, other_ref, *refs):
        weight_refs, refs = refs[:ny], refs[ny:]
        out_refs, (sums, slots) = refs[:nz], refs[nz:]
        here, core, depth_at = place_ref[0], place_ref[1], place_ref[2]
        for c in range(nc):
            for k in range(ny):
                at = pl.ds(pl.multiple_of(lax.rem(here + ny - k, ny) * rows, 128), rows)
                piece = jnp.where(core == c, own_ref[:, :, at], other_ref[:, :, at])
                term = jnp.dot(
                    piece.reshape(groups * count, rows),
                    weight_refs[k][...],
                    preferred_element_type=F32,
                )
                if k == 0:
                    sums[...] = term
                else:
                    sums[...] += term
            for x in range(nx):
                for y in range(ny):
                    for z in range(nz):
                        for t in range(2):
                            at = (x * ny + y) * count + z * per + t * seqs
                            to = ((y * 2 + t) * nx * nc + x * nc + c) * seqs
                            slots[z, to : to + seqs, :] = sums[at : at + seqs, :]
        for k in range(nz):
            out_refs[k][...] = slots[lax.rem(depth_at + k, nz)].astype(BF16)

    return call(
        kernel,
        (place, own, other, *weights),
        [jax.ShapeDtypeStruct((block, depth), BF16)] * nz,
        [pltpu.VMEM((groups * count, depth), F32), pltpu.VMEM((nz, block, depth), F32)],
        flops=2 * nc * groups * count * width * depth,
    )


def join_columns(place, blocks):
    count, rows, depth = blocks.shape

    def kernel(place_ref, blocks_ref, one_ref, two_ref, joined):
        for k in range(count):
            joined[:, k * depth : (k + 1) * depth] = blocks_ref[k].astype(F32)
        one_ref[...] = joined[: rows // 2, :].astype(BF16)
        two_ref[...] = joined[rows // 2 :, :].astype(BF16)

    shape = jax.ShapeDtypeStruct((rows // 2, count * depth), BF16)
    return call(kernel, (place, blocks), [shape] * 2, [pltpu.VMEM((rows, count * depth), F32)])


def shards(step_one, step_two, gain, w_query, w_keyval, w_out, kv_cache, lengths):
    ny, nz, nx, nc = (lax.axis_size(a) for a in ("y", "z", "x", "core"))
    narrow = nx * nc
    places = [lax.axis_index(a) for a in ("y", "core", "z", "x")]
    place = jnp.stack(places).astype(jnp.int32)
    width, query_cols = w_query.shape
    pair_cols = w_keyval.shape[1]
    size = kv_cache.shape[2] // 2
    seqs = kv_cache.shape[0]
    per = 2 * seqs
    depth = width // ny

    quarters = input_quarters(place, w_query, w_keyval, ny)
    weights = [quarters[0]] + [shift(quarters[k], "y", k) for k in range(1, ny)]

    start = ((places[3] * nc + places[1]) * width).astype(jnp.int32).reshape(1)
    mine = normalize(start, (step_one, step_two), gain, nx, nc, ny, width)
    column = lax.all_to_all(mine, "y", split_axis=0, concat_axis=0, tiled=True)
    pieces = ring_pieces(column.reshape(ny * narrow * per, depth), "z")
    keep, give = project(place, pieces, weights, pair_cols, nx, per)
    cols = keep.shape[3]
    other = lax.ppermute(give, "core", [(0, 1), (1, 0)])
    pair = add(keep, other).reshape(nx * ny, nz * per, cols)
    terms = lax.all_to_all(pair, ("x", "y"), split_axis=0, concat_axis=0, tiled=True)
    summed = sum_terms(place, terms, per)
    summed, *quarters = lax.optimization_barrier((summed, *output_quarters(place, w_out, ny)))
    out_weights = [quarters[0]] + [shift(quarters[k], "y", k) for k in range(1, ny)]
    arrived = lax.all_to_all(
        summed.reshape(nz, per, cols), "z", split_axis=0, concat_axis=0, tiled=True
    )
    arrived, out_weights[1], out_weights[-1] = lax.optimization_barrier(
        (arrived, out_weights[1], out_weights[-1])
    )
    queries = arrived[:, :, : ny * query_cols].reshape(nz, per, ny, query_cols)
    queries = queries.transpose(1, 2, 0, 3).reshape(2, seqs, HEADS, size)
    keyval = arrived[:, :, ny * query_cols : ny * (query_cols + pair_cols)]
    keyval = keyval.reshape(nz, per, ny, pair_cols)
    keyval = keyval.transpose(1, 2, 0, 3).reshape(2, seqs, 2 * size)
    attended = attend(queries, keyval, kv_cache, lengths)
    leaving = attended.reshape(per, ny, nz, query_cols).transpose(2, 0, 1, 3)
    leaving = leaving.reshape(nz, per, ny * query_cols)
    returned = lax.all_to_all(leaving, "z", split_axis=0, concat_axis=0, tiled=True)
    returned = returned.reshape(nz * per, ny * query_cols)
    returned, out_weights = lax.optimization_barrier((returned, out_weights))
    copies = jnp.broadcast_to(returned, (nx * ny, *returned.shape))
    gathered = lax.all_to_all(copies, ("x", "y"), split_axis=0, concat_axis=0, tiled=True)
    other = lax.ppermute(gathered, "core", [(0, 1), (1, 0)])
    parts = project_out(place, gathered, other, out_weights, nx, nc, seqs)
    out = ring_sum(parts, "z").reshape(ny, narrow * per, depth)
    out = lax.all_to_all(out, "y", split_axis=0, concat_axis=0, tiled=True)
    return tuple(join_columns(place, out))


def solution(mesh):
    fine = Mesh(mesh.devices.reshape(4, 8, 4, 2), ("y", "z", "x", "core"))
    wide, narrow = ("y", "z"), ("x", "core")
    return jax.shard_map(
        shards,
        mesh=fine,
        in_specs=(
            P(wide, None),
            P(wide, None),
            P(),
            P(narrow, wide),
            P(narrow, wide),
            P(wide, narrow),
            P(wide + narrow, None, None),
            P(wide + narrow),
        ),
        out_specs=(P(wide, narrow), P(wide, narrow)),
        check_vma=False,
    )
```

```python
import jax
import jax.numpy as jnp
from jax import lax
from jax.experimental import pallas as pl
from jax.experimental.pallas import tpu as pltpu
from jax.sharding import Mesh, PartitionSpec as P

HEADS = 48
EPSILON = 1e-05
NEG_FILL = -1e30
F32 = jnp.float32
BF16 = jnp.bfloat16


def attend(queries, keyval, cache, lengths):
    steps, seqs, heads, size = queries.shape
    scale = size ** (-0.5)
    rows = queries.transpose(1, 0, 2, 3).reshape(seqs, steps * heads, size)
    keys, values = cache[:, :, :size], cache[:, :, size:]
    new = keyval.transpose(1, 0, 2)
    new_keys, new_values = new[:, :, :size], new[:, :, size:]
    live = (jnp.arange(cache.shape[1])[None, :] < lengths[:, None])[:, None, :]
    step_of = jnp.repeat(jnp.arange(steps), heads)
    new_live = (jnp.arange(steps)[None, :] <= step_of[:, None])[None]
    scores = jnp.einsum("srd,smd->srm", rows, keys, preferred_element_type=F32) * scale
    extra = jnp.einsum("srd,sjd->srj", rows, new_keys, preferred_element_type=F32) * scale
    scores = jnp.where(live, scores, NEG_FILL)
    extra = jnp.where(new_live, extra, NEG_FILL)
    top = jnp.maximum(jnp.max(scores, axis=-1), jnp.max(extra, axis=-1))[..., None]
    weights = jnp.where(live, jnp.exp(scores - top), 0.0)
    extra_weights = jnp.where(new_live, jnp.exp(extra - top), 0.0)
    total = jnp.sum(weights, axis=-1) + jnp.sum(extra_weights, axis=-1)
    out = jnp.einsum("srm,smd->srd", weights.astype(BF16), values, preferred_element_type=F32)
    out = out + jnp.einsum(
        "srj,sjd->srd", extra_weights.astype(BF16), new_values, preferred_element_type=F32
    )
    out = (out / total[..., None]).astype(BF16)
    return out.reshape(seqs, steps, heads * size).transpose(1, 0, 2)


VMEM = pl.BlockSpec(memory_space=pltpu.VMEM)
SMEM = pl.BlockSpec(memory_space=pltpu.SMEM)


def call(kernel, inputs, outputs, scratch, flops=0, mib=40):
    moved = sum(a.size * a.dtype.itemsize for a in (*inputs[1:], *outputs))
    return pl.pallas_call(
        kernel,
        in_specs=[SMEM] + [VMEM] * (len(inputs) - 1),
        out_specs=[VMEM] * len(outputs),
        out_shape=outputs,
        scratch_shapes=scratch,
        compiler_params=pltpu.CompilerParams(vmem_limit_bytes=mib * 2**20),
        cost_estimate=pl.CostEstimate(flops=flops, bytes_accessed=moved, transcendentals=0),
    )(*inputs)


def normalize(start, steps, gain, nx, nc, ny, width):
    count = steps[0].shape[0]
    seqs = count // (nx * nc)
    depth = width // ny

    def kernel(start_ref, one_ref, two_ref, gain_ref, out_ref, rows):
        columns = pl.ds(pl.multiple_of(start_ref[0], 128), width)
        scales = gain_ref[:, columns]
        for t, ref in enumerate((one_ref, two_ref)):
            values = ref[...].astype(F32)
            average = jnp.mean(values, axis=-1, keepdims=True)
            variance = jnp.mean(values * values, axis=-1, keepdims=True) - average * average
            own = ref[:, columns].astype(F32)
            normed = (own - average) * lax.rsqrt(variance + EPSILON) * scales
            for n in range(nx * nc):
                x, c = n // nc, n % nc
                at = ((c * nx + x) * 2 + t) * seqs
                rows[at : at + seqs, :] = normed[n * seqs : (n + 1) * seqs]
        for k in range(ny):
            out_ref[k] = rows[:, k * depth : (k + 1) * depth].astype(BF16)

    return call(
        kernel,
        (start, *steps, gain.reshape(1, -1)),
        [jax.ShapeDtypeStruct((ny, 2 * count, depth), BF16)],
        [pltpu.VMEM((2 * count, width), F32)],
        mib=58,
    )[0]


def input_quarters(place, w_query, w_keyval, ny):
    width, cols = w_query.shape
    small = w_keyval.shape[1]
    depth = width // ny

    def kernel(place_ref, query_ref, keyval_ref, *out_refs):
        unit = (
            lax.broadcasted_iota(jnp.int32, (small, small), 0)
            == lax.broadcasted_iota(jnp.int32, (small, small), 1)
        ).astype(BF16)
        for k, out_ref in enumerate(out_refs):
            at = pl.multiple_of(lax.rem(place_ref[0] + k, ny) * depth, 16)
            out_ref[:depth, :] = query_ref[pl.ds(at, depth), :]
            turned = lax.dot_general(
                unit,
                keyval_ref[pl.ds(at, depth), :],
                (((1,), (1,)), ((), ())),
                preferred_element_type=F32,
            ).astype(BF16)
            rest = jnp.zeros((small, 2 * cols - depth), BF16)
            out_ref[depth : depth + small, :] = turned[:, :cols]
            out_ref[depth + small :, :] = jnp.concatenate([turned[:, cols:], rest], axis=1)

    shape = jax.ShapeDtypeStruct((depth + 2 * small, cols), BF16)
    return call(kernel, (place, w_query, w_keyval), [shape] * ny, [])


def output_quarters(place, w_out, ny):
    rows, width = w_out.shape
    depth = width // ny

    def kernel(place_ref, weights_ref, *refs):
        out_refs, quarters = refs[:-1], refs[-1]
        for k in range(ny):
            quarters[k] = weights_ref[:, k * depth : (k + 1) * depth]
        for k, out_ref in enumerate(out_refs):
            out_ref[...] = quarters[lax.rem(place_ref[0] + k, ny)]

    shape = jax.ShapeDtypeStruct((rows, depth), BF16)
    return call(kernel, (place, w_out), [shape] * ny, [pltpu.VMEM((ny, rows, depth), BF16)])


def shift(value, axis, by):
    count = lax.axis_size(axis)
    return lax.ppermute(value, axis, [(i, (i + by) % count) for i in range(count)])


def add(*terms):
    return sum(t.astype(F32) for t in terms).astype(BF16)


def ring_pieces(block, axis):
    half = lax.axis_size(axis) // 2
    up, down = [block], [block]
    for _ in range(half - 1):
        up.append(shift(up[-1], axis, 1))
        down.append(shift(down[-1], axis, -1))
    return down + [shift(up[-1], axis, 1)] + up[:0:-1]


def ring_sum(parts, axis):
    count = len(parts)
    half = count // 2
    up, down = shift(parts[half], axis, 1), None
    for k in range(half - 1, 0, -1):
        upper = add(parts[k], up)
        lower = parts[count - k] if down is None else add(parts[count - k], down)
        up, down = shift(upper, axis, 1), shift(lower, axis, -1)
    return add(parts[0], up, down)


def project(place, pieces, weights, small, nx, per):
    count, depth = pieces[0].shape
    ny, cols = len(weights), weights[0].shape[1]
    nz = len(pieces)
    part = nx * per
    total = ny * cols + 128
    shape = (nx, ny, nz * per, total)
    group = min(nz, 4)

    def kernel(place_ref, *refs):
        row_refs, refs = refs[:nz], refs[nz:]
        weight_refs, refs = refs[:ny], refs[ny:]
        keep_ref, give_ref, rows, smalls, sums, kept, given = refs
        here, core = place_ref[0], place_ref[1]
        smalls[...] = jnp.zeros_like(smalls)
        for k in range(ny):
            to = pl.ds(pl.multiple_of(lax.rem(here + ny - k, ny) * small, 16), small)
            smalls[to, :cols] = weight_refs[k][depth : depth + small, :]
            smalls[to, cols:] = weight_refs[k][depth + small :, : depth - cols]
        for first in range(0, nz, group):
            for p in range(group):
                rows[p * count : (p + 1) * count, :] = row_refs[first + p][...]
            for k in range(ny):
                to = pl.multiple_of(lax.rem(here + ny - k, ny) * cols, 128)
                sums[:, pl.ds(to, cols)] = jnp.dot(
                    rows[...], weight_refs[k][:depth, :], preferred_element_type=F32
                )
            sums[:, ny * cols :] = lax.dot_general(
                rows[...], smalls[...], (((1,), (1,)), ((), ())), preferred_element_type=F32
            )
            for p in range(group):
                for y in range(ny):
                    at = p * count + y * 2 * part
                    mine = sums[pl.ds(pl.multiple_of(at + core * part, 8), part), :]
                    theirs = sums[pl.ds(pl.multiple_of(at + (1 - core) * part, 8), part), :]
                    slot = (first + p) * per
                    for x in range(nx):
                        kept[x, y, slot : slot + per, :] = mine[x * per : (x + 1) * per]
                        given[x, y, slot : slot + per, :] = theirs[x * per : (x + 1) * per]
        for x in range(nx):
            keep_ref[x] = kept[x].astype(BF16)
            give_ref[x] = given[x].astype(BF16)

    return call(
        kernel,
        (place, *pieces, *weights),
        [jax.ShapeDtypeStruct(shape, BF16)] * 2,
        [
            pltpu.VMEM((group * count, depth), BF16),
            pltpu.VMEM((128, depth), BF16),
            pltpu.VMEM((group * count, total), F32),
            pltpu.VMEM(shape, F32),
            pltpu.VMEM(shape, F32),
        ],
        flops=2 * count * nz * depth * total,
    )


def add_halves(place, ones, others):
    nx, ny, rows, cols = ones[0].shape
    count = len(ones)

    def kernel(place_ref, *refs):
        out_ref = refs[-1]
        for h in range(count):
            for x in range(nx):
                for y in range(ny):
                    total = refs[h][x, y].astype(F32) + refs[count + h][x, y].astype(F32)
                    out_ref[x * ny + y, h * rows : (h + 1) * rows, :] = total.astype(BF16)

    shape = jax.ShapeDtypeStruct((nx * ny, count * rows, cols), BF16)
    return call(kernel, (place, *ones, *others), [shape], [])[0]


def sum_terms(place, terms, per, first):
    def kernel(place_ref, terms_ref, out_ref):
        total = terms_ref[0].astype(F32)
        for i in range(1, terms_ref.shape[0]):
            total = total + terms_ref[i].astype(F32)
        by = lax.rem(place_ref[2] + first, total.shape[0] // per) * per
        out_ref[...] = pltpu.roll(total, by, 0).astype(BF16)

    return call(kernel, (place, terms), [jax.ShapeDtypeStruct(terms.shape[1:], BF16)], [])[0]


def project_out(place, own, other, weights, nx, nc, seqs):
    groups, count, width = own.shape
    ny = len(weights)
    rows, depth = weights[0].shape
    per = 2 * seqs
    nz = count // per
    block = ny * 2 * nx * nc * seqs

    def kernel(place_ref, own_ref, other_ref, *refs):
        weight_refs, refs = refs[:ny], refs[ny:]
        out_refs, (sums, slots) = refs[:nz], refs[nz:]
        here, core, depth_at = place_ref[0], place_ref[1], place_ref[2]
        for c in range(nc):
            for k in range(ny):
                at = pl.ds(pl.multiple_of(lax.rem(here + ny - k, ny) * rows, 128), rows)
                piece = jnp.where(core == c, own_ref[:, :, at], other_ref[:, :, at])
                term = jnp.dot(
                    piece.reshape(groups * count, rows),
                    weight_refs[k][...],
                    preferred_element_type=F32,
                )
                if k == 0:
                    sums[...] = term
                else:
                    sums[...] += term
            for x in range(nx):
                for y in range(ny):
                    for z in range(nz):
                        for t in range(2):
                            at = (x * ny + y) * count + z * per + t * seqs
                            to = ((y * 2 + t) * nx * nc + x * nc + c) * seqs
                            slots[z, to : to + seqs, :] = sums[at : at + seqs, :]
        for k in range(nz):
            out_refs[k][...] = slots[lax.rem(depth_at + k, nz)].astype(BF16)

    return call(
        kernel,
        (place, own, other, *weights),
        [jax.ShapeDtypeStruct((block, depth), BF16)] * nz,
        [pltpu.VMEM((groups * count, depth), F32), pltpu.VMEM((nz, block, depth), F32)],
        flops=2 * nc * groups * count * width * depth,
    )


def join_columns(place, blocks):
    count, rows, depth = blocks.shape

    def kernel(place_ref, blocks_ref, one_ref, two_ref, joined):
        for k in range(count):
            joined[:, k * depth : (k + 1) * depth] = blocks_ref[k].astype(F32)
        one_ref[...] = joined[: rows // 2, :].astype(BF16)
        two_ref[...] = joined[rows // 2 :, :].astype(BF16)

    shape = jax.ShapeDtypeStruct((rows // 2, count * depth), BF16)
    return call(kernel, (place, blocks), [shape] * 2, [pltpu.VMEM((rows, count * depth), F32)])


def shards(step_one, step_two, gain, w_query, w_keyval, w_out, kv_cache, lengths):
    ny, nz, nx, nc = (lax.axis_size(a) for a in ("y", "z", "x", "core"))
    narrow = nx * nc
    places = [lax.axis_index(a) for a in ("y", "core", "z", "x")]
    place = jnp.stack(places).astype(jnp.int32)
    width, query_cols = w_query.shape
    pair_cols = w_keyval.shape[1]
    size = kv_cache.shape[2] // 2
    seqs = kv_cache.shape[0]
    per = 2 * seqs
    depth = width // ny

    start = ((places[3] * nc + places[1]) * width).astype(jnp.int32).reshape(1)
    mine = normalize(start, (step_one, step_two), gain, nx, nc, ny, width)
    column = lax.all_to_all(mine, "y", split_axis=0, concat_axis=0, tiled=True)
    w_query, column = lax.optimization_barrier((w_query, column))
    quarters = input_quarters(place, w_query, w_keyval, ny)
    weights = [quarters[0]] + [shift(quarters[k], "y", k) for k in range(1, ny)]
    pieces = ring_pieces(column.reshape(ny * narrow * per, depth), "z")
    first = nz - nz // 4
    turned = pieces[first:] + pieces[:first]
    halves = [
        project(place, half, weights, pair_cols, nx, per)
        for half in (turned[: nz // 2], turned[nz // 2 :])
    ]
    cols = halves[0][0].shape[3]
    others = [lax.ppermute(give, "core", [(0, 1), (1, 0)]) for _, give in halves]
    pair = add_halves(place, [keep for keep, _ in halves], others)
    terms = lax.all_to_all(pair, ("x", "y"), split_axis=0, concat_axis=0, tiled=True)
    summed = sum_terms(place, terms, per, first)
    summed, *quarters = lax.optimization_barrier((summed, *output_quarters(place, w_out, ny)))
    out_weights = [quarters[0]] + [shift(quarters[k], "y", k) for k in range(1, ny)]
    arrived = lax.all_to_all(
        summed.reshape(nz, per, cols), "z", split_axis=0, concat_axis=0, tiled=True
    )
    queries = arrived[:, :, : ny * query_cols].reshape(nz, per, ny, query_cols)
    queries = queries.transpose(1, 2, 0, 3).reshape(2, seqs, HEADS, size)
    keyval = arrived[:, :, ny * query_cols : ny * (query_cols + pair_cols)]
    keyval = keyval.reshape(nz, per, ny, pair_cols)
    keyval = keyval.transpose(1, 2, 0, 3).reshape(2, seqs, 2 * size)
    attended = attend(queries, keyval, kv_cache, lengths)
    leaving = attended.reshape(per, ny, nz, query_cols).transpose(2, 0, 1, 3)
    leaving = leaving.reshape(nz, per, ny * query_cols)
    returned = lax.all_to_all(leaving, "z", split_axis=0, concat_axis=0, tiled=True)
    returned = returned.reshape(nz * per, ny * query_cols)
    returned, out_weights = lax.optimization_barrier((returned, out_weights))
    copies = jnp.broadcast_to(returned, (nx * ny, *returned.shape))
    gathered = lax.all_to_all(copies, ("x", "y"), split_axis=0, concat_axis=0, tiled=True)
    other = lax.ppermute(gathered, "core", [(0, 1), (1, 0)])
    parts = project_out(place, gathered, other, out_weights, nx, nc, seqs)
    out = ring_sum(parts, "z").reshape(ny, narrow * per, depth)
    out = lax.all_to_all(out, "y", split_axis=0, concat_axis=0, tiled=True)
    return tuple(join_columns(place, out))


def solution(mesh):
    fine = Mesh(mesh.devices.reshape(4, 8, 4, 2), ("y", "z", "x", "core"))
    wide, narrow = ("y", "z"), ("x", "core")
    return jax.shard_map(
        shards,
        mesh=fine,
        in_specs=(
            P(wide, None),
            P(wide, None),
            P(),
            P(narrow, wide),
            P(narrow, wide),
            P(wide, narrow),
            P(wide + narrow, None, None),
            P(wide + narrow),
        ),
        out_specs=(P(wide, narrow), P(wide, narrow)),
        check_vma=False,
    )
```

```python
import jax
import jax.numpy as jnp
from jax import lax
from jax.experimental import pallas as pl
from jax.experimental.pallas import tpu as pltpu
from jax.sharding import Mesh, PartitionSpec as P

HEADS = 48
EPSILON = 1e-05
NEG_FILL = -1e30
F32 = jnp.float32
BF16 = jnp.bfloat16


def attend(queries, keyval, cache, lengths):
    steps, seqs, heads, size = queries.shape
    scale = size ** (-0.5)
    rows = queries.transpose(1, 0, 2, 3).reshape(seqs, steps * heads, size)
    keys, values = cache[:, :, :size], cache[:, :, size:]
    new = keyval.transpose(1, 0, 2)
    new_keys, new_values = new[:, :, :size], new[:, :, size:]
    live = (jnp.arange(cache.shape[1])[None, :] < lengths[:, None])[:, None, :]
    step_of = jnp.repeat(jnp.arange(steps), heads)
    new_live = (jnp.arange(steps)[None, :] <= step_of[:, None])[None]
    scores = jnp.einsum("srd,smd->srm", rows, keys, preferred_element_type=F32) * scale
    extra = jnp.einsum("srd,sjd->srj", rows, new_keys, preferred_element_type=F32) * scale
    scores = jnp.where(live, scores, NEG_FILL)
    extra = jnp.where(new_live, extra, NEG_FILL)
    top = jnp.maximum(jnp.max(scores, axis=-1), jnp.max(extra, axis=-1))[..., None]
    weights = jnp.where(live, jnp.exp(scores - top), 0.0)
    extra_weights = jnp.where(new_live, jnp.exp(extra - top), 0.0)
    total = jnp.sum(weights, axis=-1) + jnp.sum(extra_weights, axis=-1)
    out = jnp.einsum("srm,smd->srd", weights.astype(BF16), values, preferred_element_type=F32)
    out = out + jnp.einsum(
        "srj,sjd->srd", extra_weights.astype(BF16), new_values, preferred_element_type=F32
    )
    out = (out / total[..., None]).astype(BF16)
    return out.reshape(seqs, steps, heads * size).transpose(1, 0, 2)


VMEM = pl.BlockSpec(memory_space=pltpu.VMEM)
SMEM = pl.BlockSpec(memory_space=pltpu.SMEM)


def call(kernel, inputs, outputs, scratch, flops=0, mib=40):
    moved = sum(a.size * a.dtype.itemsize for a in (*inputs[1:], *outputs))
    return pl.pallas_call(
        kernel,
        in_specs=[SMEM] + [VMEM] * (len(inputs) - 1),
        out_specs=[VMEM] * len(outputs),
        out_shape=outputs,
        scratch_shapes=scratch,
        compiler_params=pltpu.CompilerParams(vmem_limit_bytes=mib * 2**20),
        cost_estimate=pl.CostEstimate(flops=flops, bytes_accessed=moved, transcendentals=0),
    )(*inputs)


def normalize(start, steps, gain, nx, nc, ny, width):
    count = steps[0].shape[0]
    seqs = count // (nx * nc)
    depth = width // ny

    def kernel(start_ref, one_ref, two_ref, gain_ref, out_ref, rows):
        columns = pl.ds(pl.multiple_of(start_ref[0], 128), width)
        scales = gain_ref[:, columns]
        for t, ref in enumerate((one_ref, two_ref)):
            values = ref[...].astype(F32)
            average = jnp.mean(values, axis=-1, keepdims=True)
            variance = jnp.mean(values * values, axis=-1, keepdims=True) - average * average
            own = ref[:, columns].astype(F32)
            normed = (own - average) * lax.rsqrt(variance + EPSILON) * scales
            for n in range(nx * nc):
                x, c = n // nc, n % nc
                at = ((c * nx + x) * 2 + t) * seqs
                rows[at : at + seqs, :] = normed[n * seqs : (n + 1) * seqs]
        for k in range(ny):
            out_ref[k] = rows[:, k * depth : (k + 1) * depth].astype(BF16)

    return call(
        kernel,
        (start, *steps, gain.reshape(1, -1)),
        [jax.ShapeDtypeStruct((ny, 2 * count, depth), BF16)],
        [pltpu.VMEM((2 * count, width), F32)],
        mib=58,
    )[0]


def input_quarters(place, w_query, w_keyval, ny):
    width, cols = w_query.shape
    small = w_keyval.shape[1]
    depth = width // ny

    def kernel(place_ref, query_ref, keyval_ref, *out_refs):
        unit = (
            lax.broadcasted_iota(jnp.int32, (small, small), 0)
            == lax.broadcasted_iota(jnp.int32, (small, small), 1)
        ).astype(BF16)
        for k, out_ref in enumerate(out_refs):
            at = pl.multiple_of(lax.rem(place_ref[0] + k, ny) * depth, 16)
            out_ref[:depth, :] = query_ref[pl.ds(at, depth), :]
            turned = lax.dot_general(
                unit,
                keyval_ref[pl.ds(at, depth), :],
                (((1,), (1,)), ((), ())),
                preferred_element_type=F32,
            ).astype(BF16)
            rest = jnp.zeros((small, 2 * cols - depth), BF16)
            out_ref[depth : depth + small, :] = turned[:, :cols]
            out_ref[depth + small :, :] = jnp.concatenate([turned[:, cols:], rest], axis=1)

    shape = jax.ShapeDtypeStruct((depth + 2 * small, cols), BF16)
    return call(kernel, (place, w_query, w_keyval), [shape] * ny, [])


def output_quarters(place, w_out, ny):
    rows, width = w_out.shape
    depth = width // ny

    def kernel(place_ref, weights_ref, *refs):
        out_refs, quarters = refs[:-1], refs[-1]
        for k in range(ny):
            quarters[k] = weights_ref[:, k * depth : (k + 1) * depth]
        for k, out_ref in enumerate(out_refs):
            out_ref[...] = quarters[lax.rem(place_ref[0] + k, ny)]

    shape = jax.ShapeDtypeStruct((rows, depth), BF16)
    return call(kernel, (place, w_out), [shape] * ny, [pltpu.VMEM((ny, rows, depth), BF16)])


def shift(value, axis, by):
    count = lax.axis_size(axis)
    return lax.ppermute(value, axis, [(i, (i + by) % count) for i in range(count)])


def add(*terms):
    return sum(t.astype(F32) for t in terms).astype(BF16)


def ring_pieces(block, axis):
    half = lax.axis_size(axis) // 2
    up, down = [block], [block]
    for _ in range(half - 1):
        up.append(shift(up[-1], axis, 1))
        down.append(shift(down[-1], axis, -1))
    return down + [shift(up[-1], axis, 1)] + up[:0:-1]


def ring_sum(parts, axis):
    count = len(parts)
    half = count // 2
    up, down = shift(parts[half], axis, 1), None
    for k in range(half - 1, 0, -1):
        upper = add(parts[k], up)
        lower = parts[count - k] if down is None else add(parts[count - k], down)
        up, down = shift(upper, axis, 1), shift(lower, axis, -1)
    return add(parts[0], up, down)


def project(place, pieces, weights, small, nx, per):
    count, depth = pieces[0].shape
    ny, cols = len(weights), weights[0].shape[1]
    nz = len(pieces)
    part = nx * per
    total = ny * cols + 128
    shape = (nx, ny, nz * per, total)
    group = min(nz, 4)

    def kernel(place_ref, *refs):
        row_refs, refs = refs[:nz], refs[nz:]
        weight_refs, refs = refs[:ny], refs[ny:]
        keep_ref, give_ref, rows, smalls, sums, kept, given = refs
        here, core = place_ref[0], place_ref[1]
        smalls[...] = jnp.zeros_like(smalls)
        for k in range(ny):
            to = pl.ds(pl.multiple_of(lax.rem(here + ny - k, ny) * small, 16), small)
            smalls[to, :cols] = weight_refs[k][depth : depth + small, :]
            smalls[to, cols:] = weight_refs[k][depth + small :, : depth - cols]
        for first in range(0, nz, group):
            for p in range(group):
                rows[p * count : (p + 1) * count, :] = row_refs[first + p][...]
            for k in range(ny):
                to = pl.multiple_of(lax.rem(here + ny - k, ny) * cols, 128)
                sums[:, pl.ds(to, cols)] = jnp.dot(
                    rows[...], weight_refs[k][:depth, :], preferred_element_type=F32
                )
            sums[:, ny * cols :] = lax.dot_general(
                rows[...], smalls[...], (((1,), (1,)), ((), ())), preferred_element_type=F32
            )
            for p in range(group):
                for y in range(ny):
                    at = p * count + y * 2 * part
                    mine = sums[pl.ds(pl.multiple_of(at + core * part, 8), part), :]
                    theirs = sums[pl.ds(pl.multiple_of(at + (1 - core) * part, 8), part), :]
                    slot = (first + p) * per
                    for x in range(nx):
                        kept[x, y, slot : slot + per, :] = mine[x * per : (x + 1) * per]
                        given[x, y, slot : slot + per, :] = theirs[x * per : (x + 1) * per]
        for x in range(nx):
            keep_ref[x] = kept[x].astype(BF16)
            give_ref[x] = given[x].astype(BF16)

    return call(
        kernel,
        (place, *pieces, *weights),
        [jax.ShapeDtypeStruct(shape, BF16)] * 2,
        [
            pltpu.VMEM((group * count, depth), BF16),
            pltpu.VMEM((128, depth), BF16),
            pltpu.VMEM((group * count, total), F32),
            pltpu.VMEM(shape, F32),
            pltpu.VMEM(shape, F32),
        ],
        flops=2 * count * nz * depth * total,
    )


def add_halves(place, ones, others):
    nx, ny, rows, cols = ones[0].shape
    count = len(ones)

    def kernel(place_ref, *refs):
        out_ref = refs[-1]
        for h in range(count):
            for x in range(nx):
                for y in range(ny):
                    total = refs[h][x, y].astype(F32) + refs[count + h][x, y].astype(F32)
                    out_ref[x * ny + y, h * rows : (h + 1) * rows, :] = total.astype(BF16)

    shape = jax.ShapeDtypeStruct((nx * ny, count * rows, cols), BF16)
    return call(kernel, (place, *ones, *others), [shape], [])[0]


def sum_terms(place, terms, per, first):
    def kernel(place_ref, terms_ref, out_ref):
        total = terms_ref[0].astype(F32)
        for i in range(1, terms_ref.shape[0]):
            total = total + terms_ref[i].astype(F32)
        by = lax.rem(place_ref[2] + first, total.shape[0] // per) * per
        out_ref[...] = pltpu.roll(total, by, 0).astype(BF16)

    return call(kernel, (place, terms), [jax.ShapeDtypeStruct(terms.shape[1:], BF16)], [])[0]


def multiply_rows(place, gathered, weights):
    groups, count, width = gathered.shape
    ny = len(weights)
    rows, depth = weights[0].shape

    def kernel(place_ref, rows_ref, *refs):
        weight_refs, out_ref = refs[:ny], refs[ny]
        for k in range(ny):
            at = pl.multiple_of(lax.rem(place_ref[0] + ny - k, ny) * rows, 128)
            piece = rows_ref[:, :, pl.ds(at, rows)].reshape(groups * count, rows)
            term = jnp.dot(piece, weight_refs[k][...], preferred_element_type=F32)
            if k == 0:
                out_ref[...] = term
            else:
                out_ref[...] += term

    return call(
        kernel,
        (place, gathered, *weights),
        [jax.ShapeDtypeStruct((groups * count, depth), F32)],
        [],
        flops=2 * groups * count * width * depth,
    )[0]


def arrange(place, own, other, nx, ny, nc, nz, seqs):
    depth = own.shape[1]
    per = 2 * seqs
    block = ny * 2 * nx * nc * seqs

    def kernel(place_ref, own_ref, other_ref, *refs):
        out_refs, slots = refs[:nz], refs[nz]
        core, here = place_ref[1], place_ref[2]
        for x in range(nx):
            for y in range(ny):
                at = (x * ny + y) * nz * per
                one = own_ref[at : at + nz * per, :]
                two = other_ref[at : at + nz * per, :]
                for c in range(nc):
                    rows = jnp.where(core == c, one, two)
                    for z in range(nz):
                        for t in range(2):
                            start = z * per + t * seqs
                            to = ((y * 2 + t) * nx * nc + x * nc + c) * seqs
                            slots[z, to : to + seqs, :] = rows[start : start + seqs]
        for k in range(nz):
            out_refs[k][...] = slots[lax.rem(here + k, nz)].astype(BF16)

    return call(
        kernel,
        (place, own, other),
        [jax.ShapeDtypeStruct((block, depth), BF16)] * nz,
        [pltpu.VMEM((nz, block, depth), F32)],
    )


def join_columns(place, blocks):
    count, rows, depth = blocks.shape

    def kernel(place_ref, blocks_ref, one_ref, two_ref, joined):
        for k in range(count):
            joined[:, k * depth : (k + 1) * depth] = blocks_ref[k].astype(F32)
        one_ref[...] = joined[: rows // 2, :].astype(BF16)
        two_ref[...] = joined[rows // 2 :, :].astype(BF16)

    shape = jax.ShapeDtypeStruct((rows // 2, count * depth), BF16)
    return call(kernel, (place, blocks), [shape] * 2, [pltpu.VMEM((rows, count * depth), F32)])


def shards(step_one, step_two, gain, w_query, w_keyval, w_out, kv_cache, lengths):
    ny, nz, nx, nc = (lax.axis_size(a) for a in ("y", "z", "x", "core"))
    narrow = nx * nc
    places = [lax.axis_index(a) for a in ("y", "core", "z", "x")]
    place = jnp.stack(places).astype(jnp.int32)
    width, query_cols = w_query.shape
    pair_cols = w_keyval.shape[1]
    size = kv_cache.shape[2] // 2
    seqs = kv_cache.shape[0]
    per = 2 * seqs
    depth = width // ny

    start = ((places[3] * nc + places[1]) * width).astype(jnp.int32).reshape(1)
    mine = normalize(start, (step_one, step_two), gain, nx, nc, ny, width)
    column = lax.all_to_all(mine, "y", split_axis=0, concat_axis=0, tiled=True)
    w_query, column = lax.optimization_barrier((w_query, column))
    quarters = input_quarters(place, w_query, w_keyval, ny)
    weights = [quarters[0]] + [shift(quarters[k], "y", k) for k in range(1, ny)]
    pieces = ring_pieces(column.reshape(ny * narrow * per, depth), "z")
    first = nz - nz // 4
    turned = pieces[first:] + pieces[:first]
    halves = [
        project(place, half, weights, pair_cols, nx, per)
        for half in (turned[: nz // 2], turned[nz // 2 :])
    ]
    cols = halves[0][0].shape[3]
    others = [lax.ppermute(give, "core", [(0, 1), (1, 0)]) for _, give in halves]
    pair = add_halves(place, [keep for keep, _ in halves], others)
    terms = lax.all_to_all(pair, ("x", "y"), split_axis=0, concat_axis=0, tiled=True)
    summed = sum_terms(place, terms, per, first)
    summed, *quarters = lax.optimization_barrier((summed, *output_quarters(place, w_out, ny)))
    out_weights = [quarters[0]] + [shift(quarters[k], "y", k) for k in range(1, ny)]
    arrived = lax.all_to_all(
        summed.reshape(nz, per, cols), "z", split_axis=0, concat_axis=0, tiled=True
    )
    queries = arrived[:, :, : ny * query_cols].reshape(nz, per, ny, query_cols)
    queries = queries.transpose(1, 2, 0, 3).reshape(2, seqs, HEADS, size)
    keyval = arrived[:, :, ny * query_cols : ny * (query_cols + pair_cols)]
    keyval = keyval.reshape(nz, per, ny, pair_cols)
    keyval = keyval.transpose(1, 2, 0, 3).reshape(2, seqs, 2 * size)
    attended = attend(queries, keyval, kv_cache, lengths)
    leaving = attended.reshape(per, ny, nz, query_cols).transpose(2, 0, 1, 3)
    leaving = leaving.reshape(nz, per, ny * query_cols)
    returned = lax.all_to_all(leaving, "z", split_axis=0, concat_axis=0, tiled=True)
    returned = returned.reshape(nz * per, ny * query_cols)
    returned, out_weights = lax.optimization_barrier((returned, out_weights))
    copies = jnp.broadcast_to(returned, (nx * ny, *returned.shape))
    gathered = lax.all_to_all(copies, ("x", "y"), split_axis=0, concat_axis=0, tiled=True)
    other = lax.ppermute(gathered, "core", [(0, 1), (1, 0)])
    own = multiply_rows(place, gathered, out_weights)
    other = multiply_rows(place, other, out_weights)
    parts = arrange(place, own, other, nx, ny, nc, nz, seqs)
    out = ring_sum(parts, "z").reshape(ny, narrow * per, depth)
    out = lax.all_to_all(out, "y", split_axis=0, concat_axis=0, tiled=True)
    return tuple(join_columns(place, out))


def solution(mesh):
    fine = Mesh(mesh.devices.reshape(4, 8, 4, 2), ("y", "z", "x", "core"))
    wide, narrow = ("y", "z"), ("x", "core")
    return jax.shard_map(
        shards,
        mesh=fine,
        in_specs=(
            P(wide, None),
            P(wide, None),
            P(),
            P(narrow, wide),
            P(narrow, wide),
            P(wide, narrow),
            P(wide + narrow, None, None),
            P(wide + narrow),
        ),
        out_specs=(P(wide, narrow), P(wide, narrow)),
        check_vma=False,
    )
```

```python
import jax
import jax.numpy as jnp
from jax import lax
from jax.experimental import pallas as pl
from jax.experimental.pallas import tpu as pltpu
from jax.sharding import Mesh, PartitionSpec as P

HEADS = 48
EPSILON = 1e-05
NEG_FILL = -1e30
F32 = jnp.float32
BF16 = jnp.bfloat16


def attend(queries, keyval, cache, lengths):
    steps, seqs, heads, size = queries.shape
    scale = size ** (-0.5)
    rows = queries.transpose(1, 0, 2, 3).reshape(seqs, steps * heads, size)
    keys, values = cache[:, :, :size], cache[:, :, size:]
    new = keyval.transpose(1, 0, 2)
    new_keys, new_values = new[:, :, :size], new[:, :, size:]
    live = (jnp.arange(cache.shape[1])[None, :] < lengths[:, None])[:, None, :]
    step_of = jnp.repeat(jnp.arange(steps), heads)
    new_live = (jnp.arange(steps)[None, :] <= step_of[:, None])[None]
    scores = jnp.einsum("srd,smd->srm", rows, keys, preferred_element_type=F32) * scale
    extra = jnp.einsum("srd,sjd->srj", rows, new_keys, preferred_element_type=F32) * scale
    scores = jnp.where(live, scores, NEG_FILL)
    extra = jnp.where(new_live, extra, NEG_FILL)
    top = jnp.maximum(jnp.max(scores, axis=-1), jnp.max(extra, axis=-1))[..., None]
    weights = jnp.where(live, jnp.exp(scores - top), 0.0)
    extra_weights = jnp.where(new_live, jnp.exp(extra - top), 0.0)
    total = jnp.sum(weights, axis=-1) + jnp.sum(extra_weights, axis=-1)
    out = jnp.einsum("srm,smd->srd", weights.astype(BF16), values, preferred_element_type=F32)
    out = out + jnp.einsum(
        "srj,sjd->srd", extra_weights.astype(BF16), new_values, preferred_element_type=F32
    )
    out = (out / total[..., None]).astype(BF16)
    return out.reshape(seqs, steps, heads * size).transpose(1, 0, 2)


VMEM = pl.BlockSpec(memory_space=pltpu.VMEM)
SMEM = pl.BlockSpec(memory_space=pltpu.SMEM)


def call(kernel, inputs, outputs, scratch, flops=0, mib=40):
    moved = sum(a.size * a.dtype.itemsize for a in (*inputs[1:], *outputs))
    return pl.pallas_call(
        kernel,
        in_specs=[SMEM] + [VMEM] * (len(inputs) - 1),
        out_specs=[VMEM] * len(outputs),
        out_shape=outputs,
        scratch_shapes=scratch,
        compiler_params=pltpu.CompilerParams(vmem_limit_bytes=mib * 2**20),
        cost_estimate=pl.CostEstimate(flops=flops, bytes_accessed=moved, transcendentals=0),
    )(*inputs)


def normalize(start, steps, gain, nx, nc, ny, width):
    count = steps[0].shape[0]
    seqs = count // (nx * nc)
    depth = width // ny

    def kernel(start_ref, one_ref, two_ref, gain_ref, out_ref, rows):
        columns = pl.ds(pl.multiple_of(start_ref[0], 128), width)
        scales = gain_ref[:, columns]
        for t, ref in enumerate((one_ref, two_ref)):
            values = ref[...].astype(F32)
            average = jnp.mean(values, axis=-1, keepdims=True)
            variance = jnp.mean(values * values, axis=-1, keepdims=True) - average * average
            own = ref[:, columns].astype(F32)
            normed = (own - average) * lax.rsqrt(variance + EPSILON) * scales
            for n in range(nx * nc):
                x, c = n // nc, n % nc
                at = ((c * nx + x) * 2 + t) * seqs
                rows[at : at + seqs, :] = normed[n * seqs : (n + 1) * seqs]
        for k in range(ny):
            out_ref[k] = rows[:, k * depth : (k + 1) * depth].astype(BF16)

    return call(
        kernel,
        (start, *steps, gain.reshape(1, -1)),
        [jax.ShapeDtypeStruct((ny, 2 * count, depth), BF16)],
        [pltpu.VMEM((2 * count, width), F32)],
        mib=58,
    )[0]


def input_quarters(place, w_query, w_keyval, ny):
    width, cols = w_query.shape
    small = w_keyval.shape[1]
    depth = width // ny

    def kernel(place_ref, query_ref, keyval_ref, *out_refs):
        unit = (
            lax.broadcasted_iota(jnp.int32, (small, small), 0)
            == lax.broadcasted_iota(jnp.int32, (small, small), 1)
        ).astype(BF16)
        for k, out_ref in enumerate(out_refs):
            at = pl.multiple_of(lax.rem(place_ref[0] + k, ny) * depth, 16)
            out_ref[:depth, :] = query_ref[pl.ds(at, depth), :]
            turned = lax.dot_general(
                unit,
                keyval_ref[pl.ds(at, depth), :],
                (((1,), (1,)), ((), ())),
                preferred_element_type=F32,
            ).astype(BF16)
            rest = jnp.zeros((small, 2 * cols - depth), BF16)
            out_ref[depth : depth + small, :] = turned[:, :cols]
            out_ref[depth + small :, :] = jnp.concatenate([turned[:, cols:], rest], axis=1)

    shape = jax.ShapeDtypeStruct((depth + 2 * small, cols), BF16)
    return call(kernel, (place, w_query, w_keyval), [shape] * ny, [])


def output_quarters(place, w_out, ny):
    rows, width = w_out.shape
    depth = width // ny

    def kernel(place_ref, weights_ref, *refs):
        out_refs, quarters = refs[:-1], refs[-1]
        for k in range(ny):
            quarters[k] = weights_ref[:, k * depth : (k + 1) * depth]
        for k, out_ref in enumerate(out_refs):
            out_ref[...] = quarters[lax.rem(place_ref[0] + k, ny)]

    shape = jax.ShapeDtypeStruct((rows, depth), BF16)
    return call(kernel, (place, w_out), [shape] * ny, [pltpu.VMEM((ny, rows, depth), BF16)])


def shift(value, axis, by):
    count = lax.axis_size(axis)
    return lax.ppermute(value, axis, [(i, (i + by) % count) for i in range(count)])


def add(*terms):
    return sum(t.astype(F32) for t in terms).astype(BF16)


def ring_pieces(block, axis):
    half = lax.axis_size(axis) // 2
    up, down = [block], [block]
    for _ in range(half - 1):
        up.append(shift(up[-1], axis, 1))
        down.append(shift(down[-1], axis, -1))
    return down + [shift(up[-1], axis, 1)] + up[:0:-1]


def ring_sum(parts, axis):
    count = len(parts)
    half = count // 2
    up, down = shift(parts[half], axis, 1), None
    for k in range(half - 1, 0, -1):
        upper = add(parts[k], up)
        lower = parts[count - k] if down is None else add(parts[count - k], down)
        up, down = shift(upper, axis, 1), shift(lower, axis, -1)
    return add(parts[0], up, down)


def project(place, pieces, weights, small, nx, per):
    count, depth = pieces[0].shape
    ny, cols = len(weights), weights[0].shape[1]
    nz = len(pieces)
    part = nx * per
    total = ny * cols + 128
    shape = (nx, ny, nz * per, total)
    group = min(nz, 4)

    def kernel(place_ref, *refs):
        row_refs, refs = refs[:nz], refs[nz:]
        weight_refs, refs = refs[:ny], refs[ny:]
        keep_ref, give_ref, rows, smalls, sums, kept, given = refs
        here, core = place_ref[0], place_ref[1]
        smalls[...] = jnp.zeros_like(smalls)
        for k in range(ny):
            to = pl.ds(pl.multiple_of(lax.rem(here + ny - k, ny) * small, 16), small)
            smalls[to, :cols] = weight_refs[k][depth : depth + small, :]
            smalls[to, cols:] = weight_refs[k][depth + small :, : depth - cols]
        for first in range(0, nz, group):
            for p in range(group):
                rows[p * count : (p + 1) * count, :] = row_refs[first + p][...]
            for k in range(ny):
                to = pl.multiple_of(lax.rem(here + ny - k, ny) * cols, 128)
                sums[:, pl.ds(to, cols)] = jnp.dot(
                    rows[...], weight_refs[k][:depth, :], preferred_element_type=F32
                )
            sums[:, ny * cols :] = lax.dot_general(
                rows[...], smalls[...], (((1,), (1,)), ((), ())), preferred_element_type=F32
            )
            for p in range(group):
                for y in range(ny):
                    at = p * count + y * 2 * part
                    mine = sums[pl.ds(pl.multiple_of(at + core * part, 8), part), :]
                    theirs = sums[pl.ds(pl.multiple_of(at + (1 - core) * part, 8), part), :]
                    slot = (first + p) * per
                    for x in range(nx):
                        kept[x, y, slot : slot + per, :] = mine[x * per : (x + 1) * per]
                        given[x, y, slot : slot + per, :] = theirs[x * per : (x + 1) * per]
        for x in range(nx):
            keep_ref[x] = kept[x].astype(BF16)
            give_ref[x] = given[x].astype(BF16)

    return call(
        kernel,
        (place, *pieces, *weights),
        [jax.ShapeDtypeStruct(shape, BF16)] * 2,
        [
            pltpu.VMEM((group * count, depth), BF16),
            pltpu.VMEM((128, depth), BF16),
            pltpu.VMEM((group * count, total), F32),
            pltpu.VMEM(shape, F32),
            pltpu.VMEM(shape, F32),
        ],
        flops=2 * count * nz * depth * total,
    )


def add_halves(place, ones, others):
    nx, ny, rows, cols = ones[0].shape
    count = len(ones)

    def kernel(place_ref, *refs):
        out_ref = refs[-1]
        for h in range(count):
            for x in range(nx):
                for y in range(ny):
                    total = refs[h][x, y].astype(F32) + refs[count + h][x, y].astype(F32)
                    out_ref[x * ny + y, h * rows : (h + 1) * rows, :] = total.astype(BF16)

    shape = jax.ShapeDtypeStruct((nx * ny, count * rows, cols), BF16)
    return call(kernel, (place, *ones, *others), [shape], [])[0]


def sum_terms(place, terms, per, first):
    def kernel(place_ref, terms_ref, out_ref):
        total = terms_ref[0].astype(F32)
        for i in range(1, terms_ref.shape[0]):
            total = total + terms_ref[i].astype(F32)
        by = lax.rem(place_ref[2] + first, total.shape[0] // per) * per
        out_ref[...] = pltpu.roll(total, by, 0).astype(BF16)

    return call(kernel, (place, terms), [jax.ShapeDtypeStruct(terms.shape[1:], BF16)], [])[0]


def multiply_rows(place, gathered, weights):
    groups, count, width = gathered.shape
    ny = len(weights)
    rows, depth = weights[0].shape

    def kernel(place_ref, rows_ref, *refs):
        weight_refs, out_ref = refs[:ny], refs[ny]
        for k in range(ny):
            at = pl.multiple_of(lax.rem(place_ref[0] + ny - k, ny) * rows, 128)
            piece = rows_ref[:, :, pl.ds(at, rows)].reshape(groups * count, rows)
            term = jnp.dot(piece, weight_refs[k][...], preferred_element_type=F32)
            if k == 0:
                out_ref[...] = term
            else:
                out_ref[...] += term

    return call(
        kernel,
        (place, gathered, *weights),
        [jax.ShapeDtypeStruct((groups * count, depth), F32)],
        [],
        flops=2 * groups * count * width * depth,
    )[0]


def arrange(place, own, other, nx, ny, nc, nz, seqs):
    depth = own.shape[1]
    per = 2 * seqs
    block = ny * 2 * nx * nc * seqs

    def kernel(place_ref, own_ref, other_ref, *refs):
        out_refs, slots = refs[:nz], refs[nz]
        core, here = place_ref[1], place_ref[2]
        for x in range(nx):
            for y in range(ny):
                at = (x * ny + y) * nz * per
                one = own_ref[at : at + nz * per, :]
                two = other_ref[at : at + nz * per, :]
                for c in range(nc):
                    rows = jnp.where(core == c, one, two)
                    for z in range(nz):
                        for t in range(2):
                            start = z * per + t * seqs
                            to = ((y * 2 + t) * nx * nc + x * nc + c) * seqs
                            slots[z, to : to + seqs, :] = rows[start : start + seqs]
        for k in range(nz):
            out_refs[k][...] = slots[lax.rem(here + k, nz)].astype(BF16)

    return call(
        kernel,
        (place, own, other),
        [jax.ShapeDtypeStruct((block, depth), BF16)] * nz,
        [pltpu.VMEM((nz, block, depth), F32)],
    )


def join_columns(place, blocks):
    count, rows, depth = blocks.shape

    def kernel(place_ref, blocks_ref, one_ref, two_ref, joined):
        for k in range(count):
            joined[:, k * depth : (k + 1) * depth] = blocks_ref[k].astype(F32)
        one_ref[...] = joined[: rows // 2, :].astype(BF16)
        two_ref[...] = joined[rows // 2 :, :].astype(BF16)

    shape = jax.ShapeDtypeStruct((rows // 2, count * depth), BF16)
    return call(kernel, (place, blocks), [shape] * 2, [pltpu.VMEM((rows, count * depth), F32)])


def shards(step_one, step_two, gain, w_query, w_keyval, w_out, kv_cache, lengths):
    ny, nz, nx, nc = (lax.axis_size(a) for a in ("y", "z", "x", "core"))
    narrow = nx * nc
    places = [lax.axis_index(a) for a in ("y", "core", "z", "x")]
    place = jnp.stack(places).astype(jnp.int32)
    width, query_cols = w_query.shape
    pair_cols = w_keyval.shape[1]
    size = kv_cache.shape[2] // 2
    seqs = kv_cache.shape[0]
    per = 2 * seqs
    depth = width // ny

    start = ((places[3] * nc + places[1]) * width).astype(jnp.int32).reshape(1)
    mine = normalize(start, (step_one, step_two), gain, nx, nc, ny, width)
    w_query, mine = lax.optimization_barrier((w_query, mine))
    column = lax.all_to_all(mine, "y", split_axis=0, concat_axis=0, tiled=True)
    quarters = input_quarters(place, w_query, w_keyval, ny)
    weights = [quarters[0]] + [shift(quarters[k], "y", k) for k in range(1, ny)]
    pieces = ring_pieces(column.reshape(ny * narrow * per, depth), "z")
    first = nz - nz // 4
    turned = pieces[first:] + pieces[:first]
    halves = [
        project(place, half, weights, pair_cols, nx, per)
        for half in (turned[: nz // 2], turned[nz // 2 :])
    ]
    cols = halves[0][0].shape[3]
    others = [lax.ppermute(give, "core", [(0, 1), (1, 0)]) for _, give in halves]
    pair = add_halves(place, [keep for keep, _ in halves], others)
    terms = lax.all_to_all(pair, ("x", "y"), split_axis=0, concat_axis=0, tiled=True)
    summed = sum_terms(place, terms, per, first)
    summed, *quarters = lax.optimization_barrier((summed, *output_quarters(place, w_out, ny)))
    out_weights = [quarters[0]] + [shift(quarters[k], "y", k) for k in range(1, ny)]
    arrived = lax.all_to_all(
        summed.reshape(nz, per, cols), "z", split_axis=0, concat_axis=0, tiled=True
    )
    queries = arrived[:, :, : ny * query_cols].reshape(nz, per, ny, query_cols)
    queries = queries.transpose(1, 2, 0, 3).reshape(2, seqs, HEADS, size)
    keyval = arrived[:, :, ny * query_cols : ny * (query_cols + pair_cols)]
    keyval = keyval.reshape(nz, per, ny, pair_cols)
    keyval = keyval.transpose(1, 2, 0, 3).reshape(2, seqs, 2 * size)
    attended = attend(queries, keyval, kv_cache, lengths)
    leaving = attended.reshape(per, ny, nz, query_cols).transpose(2, 0, 1, 3)
    leaving = leaving.reshape(nz, per, ny * query_cols)
    returned = lax.all_to_all(leaving, "z", split_axis=0, concat_axis=0, tiled=True)
    returned = returned.reshape(nz * per, ny * query_cols)
    returned, out_weights = lax.optimization_barrier((returned, out_weights))
    copies = jnp.broadcast_to(returned, (nx * ny, *returned.shape))
    gathered = lax.all_to_all(copies, ("x", "y"), split_axis=0, concat_axis=0, tiled=True)
    other = lax.ppermute(gathered, "core", [(0, 1), (1, 0)])
    own = multiply_rows(place, gathered, out_weights)
    other = multiply_rows(place, other, out_weights)
    parts = arrange(place, own, other, nx, ny, nc, nz, seqs)
    out = ring_sum(parts, "z").reshape(ny, narrow * per, depth)
    out = lax.all_to_all(out, "y", split_axis=0, concat_axis=0, tiled=True)
    return tuple(join_columns(place, out))


def solution(mesh):
    fine = Mesh(mesh.devices.reshape(4, 8, 4, 2), ("y", "z", "x", "core"))
    wide, narrow = ("y", "z"), ("x", "core")
    return jax.shard_map(
        shards,
        mesh=fine,
        in_specs=(
            P(wide, None),
            P(wide, None),
            P(),
            P(narrow, wide),
            P(narrow, wide),
            P(wide, narrow),
            P(wide + narrow, None, None),
            P(wide + narrow),
        ),
        out_specs=(P(wide, narrow), P(wide, narrow)),
        check_vma=False,
    )
```
